512 devices in a mesh: doc: 16 (over x_lo, z), layer: 32 (over x_hi, y, core).
Axes of the slice: x: 4 (x_hi: 2, x_lo: 2; x = x_hi * 2 + x_lo), y: 8, z: 8, core: 2. Of those that a mesh axis runs over, the one named last changes fastest.
Arguments:
- grads: bfloat16 [8192, 32, 4096], P('doc', 'layer'), may hold values from -341 to 341
- queries: bfloat16 [1024, 32, 4096], P('doc', 'layer'), may hold values from -6 to 6
- precond: float32 [32, 4096], P('layer'), may hold values from 0.1 to 9
Outputs:
- scores: float32 [1024, 8192], P('layer', 'doc')
The draws below stay inside these ranges and needn't reach their ends.
All inputs are finite; a program needn't handle non-finite values.
Results may differ from the reference program's by a relative error of at most 0.0029.
Values may be sent and summed in bfloat16 or wider, within the bound.
A program may use at most 64 MiB of HBM per device.

```python
import math
import jax
import jax.numpy as jnp
from jax import lax

P_SIZE = 4096
LAYERS = 32
DOCS = 8192
QUERIES = 1024


def draw_grads(key, part):
    key = jax.random.fold_in(key, 11)
    k_base, k_row, k_col = jax.random.split(key, 3)
    shape = (DOCS, LAYERS, P_SIZE)
    ramp_index = jnp.arange(LAYERS).astype(jnp.float32) / max(LAYERS - 1, 1)
    base = jax.random.truncated_normal(k_base, -5.0, 5.0, shape, jnp.float32)
    ramp = jnp.exp(ramp_index * math.log(3.0))
    row = 0.3 * jnp.exp(jax.random.uniform(k_row, (DOCS, 1, 1), jnp.float32) * math.log(10.0))
    col = 0.3 * jnp.exp(jax.random.uniform(k_col, (1, LAYERS, P_SIZE), jnp.float32) * math.log(10.0))
    return (base * row * col * ramp[None, :, None]).astype(jnp.bfloat16)


def draw_precond(key, part):
    key = jax.random.fold_in(key, 23)
    ramp_index = jnp.arange(LAYERS).astype(jnp.float32) / max(LAYERS - 1, 1)
    spread = jax.random.uniform(key, (LAYERS, P_SIZE), jnp.float32)
    ramp = jnp.exp(ramp_index * math.log(3.0))
    return 0.1 * jnp.exp(spread * math.log(10.0)) * ramp[:, None]


def shard_levels(own_key, shape, cuts, low, top_value):
    factor_of = 1.0
    for dim, blocks in cuts:
        steps = jax.random.uniform(jax.random.fold_in(jax.random.fold_in(own_key, 6), dim), (blocks,), jnp.float32, low / len(cuts), top_value / len(cuts))
        factor_of = factor_of * jnp.repeat(jnp.exp(steps), shape[dim] // blocks).reshape((-1,) + (1,) * (len(shape) - 1 - dim))
    return factor_of


def normal_values(own_key, dims, scale, reach, shards=(), held_as=jnp.bfloat16):
    result = jax.random.normal(own_key, dims, jnp.float32) * scale
    if len(shards) > 0:
        result = shard_levels(own_key, dims, shards, -0.22, 0.18) * result
    return jnp.clip(result, min=-reach, max=reach).astype(held_as)


def setup_inputs(seed: int = 0) -> dict:
    key_of = jax.random.split(jax.random.key(seed), 4)
    return {
        "grads": draw_grads(jax.random.fold_in(key_of[3], 71), 0),
        "queries": normal_values(key_of[1], (QUERIES, LAYERS, P_SIZE), 1.0, 6.0, ((0, 16), (1, 32))),
        "precond": draw_precond(jax.random.fold_in(key_of[3], 71), 0),
    }


def reference(grads, queries, precond):
    pre_queries = (queries.astype(jnp.float32) * precond[None, :, :]).astype(jnp.bfloat16)
    start_dots = jnp.zeros((QUERIES, DOCS), jnp.float32)
    start_doc = jnp.zeros((DOCS,), jnp.float32)
    start_query = jnp.zeros((QUERIES,), jnp.float32)

    def one_layer(carry, layer_index):
        dots, doc_sq, query_sq = carry
        layer_grads = lax.dynamic_index_in_dim(grads, layer_index, 1, keepdims=False)
        layer_query = lax.dynamic_index_in_dim(pre_queries, layer_index, 1, keepdims=False)
        dots = dots + jnp.dot(layer_query, layer_grads.T, preferred_element_type=jnp.float32)
        doc_sq = doc_sq + lax.optimization_barrier(jnp.sum(jnp.square(layer_grads.astype(jnp.float32)), axis=1))
        query_sq = query_sq + lax.optimization_barrier(jnp.sum(jnp.square(layer_query.astype(jnp.float32)), axis=1))
        return ((dots, doc_sq, query_sq), None)
    carry, unused = lax.scan(one_layer, (start_dots, start_doc, start_query), jnp.arange(LAYERS).astype(jnp.int32))
    dots, doc_sq, query_sq = carry
    factor = math.sqrt(LAYERS * P_SIZE)
    scores = factor * dots * lax.rsqrt(query_sq + 1e-06)[:, None] * lax.rsqrt(doc_sq + 1e-06)[None, :]
    return scores
```

```python
import functools
import math

import jax
import jax.numpy as jnp
from jax import lax
from jax.experimental import pallas as pl
from jax.experimental.pallas import tpu as pltpu
from jax.sharding import PartitionSpec as P

MESH = pl.DeviceIdType.MESH
NT = (((1,), (1,)), ((), ()))
CHUNK = 16
EXTRA = 128

SLOTS = (
    (0, 0), (0, -1), (0, 1), (1, 0), (0, -2), (0, 2), (0, -3), (0, 3),
    (0, 4), (1, -3), (1, 3), (1, -1), (1, 1), (1, -2), (1, 2), (1, 4),
)


def kernel(
    n_doc, n_layer, factor,
    g_hbm, q_ref, pc_ref, out_ref,
    g, gath, part, cx, rs_out, rs_in, ds_part, ds_cx, ds_out, ds_in,
    g_sem, ag_send, ag_recv, cx_send, cx_recv, rs_send, rs_recv, dsc_send, dsc_recv, ds_send, ds_recv,
):
    n_z = n_doc // 2
    chips = n_layer // 2
    docs, width = g.shape
    rows = q_ref.shape[0]
    half = rows // 2
    n_chunks = rows // CHUNK
    mid = n_chunks // 2
    doc = lax.axis_index("doc")
    layer = lax.axis_index("layer")
    col = doc // n_z
    z = lax.rem(doc, n_z)
    chip = layer // 2
    core = lax.rem(layer, 2)

    def doc_at(other, dz):
        c = (1 - col) if other else col
        return c * n_z + lax.rem(z + (dz + n_z), n_z)

    up = (doc_at(0, 1), layer)
    down = (doc_at(0, -1), layer)
    across = (doc_at(1, 0), layer)
    twin = (doc, 2 * chip + 1 - core)

    def chip_dev(c):
        return (doc, 2 * c + core)

    barrier = pltpu.get_barrier_semaphore()
    for dev in (up, down, across, twin):
        pl.semaphore_signal(barrier, inc=1, device_id=dev, device_id_type=MESH)

    def greet(k, carry):
        pl.semaphore_signal(barrier, inc=1, device_id=chip_dev(lax.rem(chip + k, chips)), device_id_type=MESH)
        return carry

    lax.fori_loop(1, chips, greet, 0)

    load = pltpu.make_async_copy(g_hbm, g, g_sem)
    load.start()
    gath[0] = (q_ref[...].astype(jnp.float32) * pc_ref[...]).astype(jnp.bfloat16)
    pl.semaphore_wait(barrier, 4 + chips - 1)

    def piece(slot, c):
        return gath.at[slot, pl.ds(c * CHUNK, CHUNK), :]

    def send(src, dst, c, dev):
        pltpu.make_async_remote_copy(
            src_ref=piece(src, c), dst_ref=piece(dst, c), send_sem=ag_send, recv_sem=ag_recv.at[dst, c],
            device_id=dev, device_id_type=MESH,
        ).start()

    def arrived(slot, c):
        pltpu.make_async_copy(piece(slot, c), piece(slot, c), ag_recv.at[slot, c]).wait()

    def multiply(first, last):
        n = last - first
        x = gath[first:last].reshape(n * rows, width)
        dots = lax.dot_general(x, g[...], NT, preferred_element_type=jnp.float32)
        part[first:last, :, :, :docs] = dots.reshape(n, 2, half, docs)
        for s in range(first, last):
            v = gath[s].astype(jnp.float32)
            sq = jnp.sum(v * v, axis=1, keepdims=True)
            part[s, :, :, docs:] = jnp.broadcast_to(sq, (rows, EXTRA)).reshape(2, half, EXTRA)
        for s in range(first, last):
            pltpu.make_async_remote_copy(
                src_ref=part.at[s, 1 - core], dst_ref=cx.at[s], send_sem=cx_send, recv_sem=cx_recv.at[s],
                device_id=twin, device_id_type=MESH,
            ).start()

    def reduce_out(first, last):
        for s in range(first, last):
            pltpu.make_async_copy(cx.at[s], cx.at[s], cx_recv.at[s]).wait()
            v = part[s, core] + cx[s]
            dots = v[:, :docs].astype(jnp.bfloat16)
            sq = v[:, docs:]
            high = sq.astype(jnp.bfloat16)
            low = (sq - high.astype(jnp.float32)).astype(jnp.bfloat16)
            lane = lax.broadcasted_iota(jnp.int32, sq.shape, 1)
            both = jnp.where(lane < EXTRA // 2, high.astype(jnp.float32), low.astype(jnp.float32))
            rs_out[s, :, :docs] = dots
            rs_out[s, :, docs:] = both.astype(jnp.bfloat16)
            owner = doc_at(*SLOTS[s])

            @pl.when(owner != chip)
            def _():
                pltpu.make_async_remote_copy(
                    src_ref=rs_out.at[s], dst_ref=rs_in.at[chip], send_sem=rs_send, recv_sem=rs_recv,
                    device_id=chip_dev(owner), device_id_type=MESH,
                ).start()

            @pl.when(owner == chip)
            def _():
                rs_in[chip] = rs_out[s]

    chunks = range(n_chunks)
    for c in chunks:
        send(0, 1, c, up)
        send(0, 2, c, down)
        send(0, 3, c, across)

    load.wait()
    sq_rows = 64
    acc_rows = []
    for i in range(docs // sq_rows):
        acc = jnp.zeros((sq_rows, 128), jnp.float32)
        for k in range(width // 128):
            v = g[i * sq_rows : (i + 1) * sq_rows, k * 128 : (k + 1) * 128].astype(jnp.float32)
            acc = acc + v * v
        acc_rows.append(acc)
    lanes = jnp.concatenate(acc_rows, axis=0)
    ones = jnp.ones((8, 128), jnp.float32)
    doc_sq = lax.dot_general(ones, lanes, NT, preferred_element_type=jnp.float32, precision=lax.Precision.HIGHEST)
    ds_part[...] = doc_sq[0:1]
    pltpu.make_async_remote_copy(
        src_ref=ds_part, dst_ref=ds_cx, send_sem=dsc_send, recv_sem=dsc_recv, device_id=twin, device_id_type=MESH
    ).start()

    for c in chunks:
        arrived(1, c)
        send(1, 4, c, up)
        arrived(2, c)
        send(2, 5, c, down)
    for c in chunks:
        arrived(3, c)
    multiply(0, 4)

    pltpu.make_async_copy(ds_cx, ds_cx, dsc_recv).wait()
    ds_out[...] = ds_part[...] + ds_cx[...]
    ds_in[chip] = ds_out[...]

    def spread(k, carry):
        pltpu.make_async_remote_copy(
            src_ref=ds_out, dst_ref=ds_in.at[chip], send_sem=ds_send, recv_sem=ds_recv,
            device_id=chip_dev(lax.rem(chip + k, chips)), device_id_type=MESH,
        ).start()
        return carry

    lax.fori_loop(1, chips, spread, 0)

    for c in chunks:
        arrived(4, c)
        send(4, 6, c, up)
        arrived(5, c)
        send(5, 7, c, down)
        if c < mid:
            send(4, 13, c, across)
            send(5, 14, c, across)
    multiply(4, 6)
    reduce_out(0, 4)

    for c in chunks:
        arrived(6, c)
        if c < mid:
            send(6, 8, c, up)
        send(6, 9, c, across)
        arrived(7, c)
        if c >= mid:
            send(7, 8, c, down)
        send(7, 10, c, across)
    late = tuple(range(mid, n_chunks))
    early = tuple(range(mid))
    for c in late + early:
        send(3, 11, c, up)
        send(3, 12, c, down)
    multiply(6, 8)
    reduce_out(4, 6)

    for c in chunks:
        arrived(8, c)
        send(8, 15, c, across)
    for c in late:
        arrived(11, c)
        send(11, 13, c, up)
        arrived(12, c)
        send(12, 14, c, down)
    for c in chunks:
        arrived(9, c)
        arrived(10, c)
    multiply(8, 11)
    reduce_out(6, 8)
    for c in early:
        arrived(11, c)
        arrived(12, c)
    multiply(11, 13)
    reduce_out(8, 11)
    for c in chunks:
        arrived(13, c)
        arrived(14, c)
        arrived(15, c)
    multiply(13, 16)
    reduce_out(11, 13)
    reduce_out(13, 16)

    def taken(ref, sem):
        pltpu.make_async_copy(ref, ref, sem).wait()

    taken(ds_in.at[pl.ds(0, chips - 1)], ds_recv)
    doc_total = jnp.sum(ds_in[...], axis=0)
    taken(rs_in.at[pl.ds(0, chips - 1)], rs_recv)
    total = rs_in[0].astype(jnp.float32)
    for k in range(1, chips):
        total = total + rs_in[k].astype(jnp.float32)
    query_sq = total[:, docs : docs + 1] + total[:, docs + EXTRA // 2 : docs + EXTRA // 2 + 1]
    out_ref[...] = (
        factor * total[:, :docs] * lax.rsqrt(query_sq + 1e-06) * lax.rsqrt(doc_total + 1e-06)
    )

    taken(gath.at[pl.ds(0, n_doc - 1)], ag_send)
    taken(cx, cx_send)
    taken(rs_out.at[pl.ds(0, chips - 1)], rs_send)
    taken(ds_cx, dsc_send)
    taken(ds_in.at[pl.ds(0, chips - 1)], ds_send)


def shards(grads, queries, precond):
    n_doc = lax.axis_size("doc")
    n_layer = lax.axis_size("layer")
    docs, width = grads.shape[0], grads.shape[2]
    rows = queries.shape[0]
    half = rows // 2
    chips = n_layer // 2
    own_rows = rows * n_doc // n_layer
    factor = math.sqrt(n_layer * width)
    dma = pltpu.SemaphoreType.DMA
    return pl.pallas_call(
        functools.partial(kernel, n_doc, n_layer, factor),
        out_shape=jax.ShapeDtypeStruct((own_rows, docs), jnp.float32),
        in_specs=[
            pl.BlockSpec(memory_space=pl.ANY),
            pl.BlockSpec(memory_space=pltpu.VMEM),
            pl.BlockSpec(memory_space=pltpu.VMEM),
        ],
        out_specs=pl.BlockSpec(memory_space=pltpu.VMEM),
        scratch_shapes=[
            pltpu.VMEM((docs, width), jnp.bfloat16),
            pltpu.VMEM((n_doc, rows, width), jnp.bfloat16),
            pltpu.VMEM((n_doc, 2, half, docs + EXTRA), jnp.float32),
            pltpu.VMEM((n_doc, half, docs + EXTRA), jnp.float32),
            pltpu.VMEM((n_doc, half, docs + EXTRA), jnp.bfloat16),
            pltpu.VMEM((chips, half, docs + EXTRA), jnp.bfloat16),
            pltpu.VMEM((1, docs), jnp.float32),
            pltpu.VMEM((1, docs), jnp.float32),
            pltpu.VMEM((1, docs), jnp.float32),
            pltpu.VMEM((chips, 1, docs), jnp.float32),
            dma, dma, dma((n_doc, rows // CHUNK)), dma, dma((n_doc,)), dma, dma, dma, dma, dma, dma,
        ],
        compiler_params=pltpu.CompilerParams(
            collective_id=0, has_side_effects=True, vmem_limit_bytes=48 << 20
        ),
        cost_estimate=pl.CostEstimate(
            flops=2 * rows * n_doc * docs * width, bytes_accessed=2 * docs * width, transcendentals=0
        ),
        name="gather_multiply_reduce",
    )(grads.reshape(docs, width), queries.reshape(rows, width), precond)


def solution(mesh):
    placed = (P("doc", "layer", None), P("doc", "layer", None), P("layer", None))
    return jax.shard_map(
        shards, mesh=mesh, in_specs=placed, out_specs=P("layer", "doc"), check_vma=False
    )
```

```python
import functools
import math

import jax
import jax.numpy as jnp
from jax import lax
from jax.experimental import pallas as pl
from jax.experimental.pallas import tpu as pltpu
from jax.sharding import PartitionSpec as P

MESH = pl.DeviceIdType.MESH
NT = (((1,), (1,)), ((), ()))
F32 = jnp.float32
BF16 = jnp.bfloat16

OFFSETS = (0, -1, 1, -2, 2, -3, 3, 4)
UP = (1, 3, 5, 7)
DOWN = (2, 4, 6, 7)
EXTRA = 128
PIECES = 4


def kernel(
    n_doc, n_layer, swap, factor,
    g_hbm, q_hbm, pc_hbm, out_ref,
    g_own, g_send, g_oth, q_own, q_oth, pc_own, pc_oth, gath, px, part, cx, rs_out, rs_in, total, fx,
    ds_part, ds_cx, ds_out, ds_in,
    load, ag_send, ag_recv, x_send, gx_send, gx_recv, cx_send, cx_recv, rs_send, rs_recv, fx_send, fx_recv,
    dsc_send, dsc_recv, ds_send, ds_recv,
):
    n_z = n_doc // 2
    chips = n_layer // 2
    n_y = chips // 2
    docs, keep = g_own.shape
    shared = keep - swap
    rows = q_own.shape[0]
    sub = rows // 4
    piece = docs // PIECES
    doc = lax.axis_index("doc")
    layer = lax.axis_index("layer")
    col = doc // n_z
    z = lax.rem(doc, n_z)
    core = lax.rem(layer, 2)
    chip = layer // 2
    x_hi = chip // n_y
    y = lax.rem(chip, n_y)

    def doc_at(c, dz):
        return c * n_z + lax.rem(z + (dz + n_z), n_z)

    def chip_dev(c):
        return (doc, 2 * c + core)

    up = (doc_at(col, 1), layer)
    down = (doc_at(col, -1), layer)
    across = (doc_at(1 - col, 0), layer)
    twin = (doc, 2 * chip + 1 - core)
    far = (doc_at(1 - col, 0), 2 * ((1 - x_hi) * n_y + y) + core)

    barrier = pltpu.get_barrier_semaphore()
    for dev in (up, down, across, twin, far):
        pl.semaphore_signal(barrier, inc=1, device_id=dev, device_id_type=MESH)

    def greet(k, carry):
        pl.semaphore_signal(barrier, inc=1, device_id=chip_dev(lax.rem(chip + k, chips)), device_id_type=MESH)
        return carry

    lax.fori_loop(1, chips, greet, 0)

    mine = pl.ds(pl.multiple_of(col * swap, 128), swap)
    theirs = pl.ds(pl.multiple_of((1 - col) * swap, 128), swap)
    common = pl.ds(2 * swap, shared)
    first, rest = pl.ds(0, swap), pl.ds(swap, shared)
    loads = [
        (q_hbm.at[:, mine], q_own.at[:, first]),
        (q_hbm.at[:, common], q_own.at[:, rest]),
        (q_hbm.at[:, theirs], q_oth),
        (pc_hbm.at[:, mine], pc_own.at[:, first]),
        (pc_hbm.at[:, common], pc_own.at[:, rest]),
        (pc_hbm.at[:, theirs], pc_oth),
    ]
    n_small = len(loads)
    for i in range(PIECES):
        r = pl.ds(i * piece, piece)
        loads.append((g_hbm.at[r, theirs], g_send.at[r]))
    loads.append((g_hbm.at[:, mine], g_own.at[:, first]))
    loads.append((g_hbm.at[:, common], g_own.at[:, rest]))
    loads = [pltpu.make_async_copy(src, dst, load.at[i]) for i, (src, dst) in enumerate(loads)]
    for copy in loads:
        copy.start()
    for copy in loads[:n_small]:
        copy.wait()
    pre_own = (q_own[...].astype(F32) * pc_own[...]).astype(BF16)
    pre_oth = (q_oth[...].astype(F32) * pc_oth[...]).astype(BF16)
    for p in range(2):
        for k in range(2):
            r = slice((2 * k + p) * sub, (2 * k + p + 1) * sub)
            gath[p, 0, 0, k] = pre_own[r]
            px[p, k, :, :swap] = pre_oth[r]
            px[p, k, :, swap:] = pre_own[r, swap:]
    pl.semaphore_wait(barrier, 5 + chips - 1)

    def wait_for(ref, sem):
        pltpu.make_async_copy(ref, ref, sem).wait()

    seen = set()
    whole = set()

    def block(p, place, o, k=None):
        return gath.at[p, place, o] if k is None else gath.at[p, place, o, k]

    def send(p, src, dst, o, k, dev):
        pltpu.make_async_remote_copy(
            src_ref=block(p, src, o, k), dst_ref=block(p, dst, o, k),
            send_sem=ag_send, recv_sem=ag_recv.at[p, dst, o, k or 0], device_id=dev, device_id_type=MESH,
        ).start()

    def arrived(p, place, o, k):
        k = None if (p, place, o) in whole else k
        if (p, place, o, k) not in seen and (place, o) != (0, 0):
            seen.add((p, place, o, k))
            wait_for(block(p, place, o, k), ag_recv.at[p, place, o, k or 0])

    def pass_on(o, hops, p, split=False):
        for dev, way, first in ((up, UP, 0), (down, DOWN, 1)):
            here = way[hops - 1] if hops else 0
            if hops == 3 or split:
                for k in (first, 1 - first) if hops < 3 else (first,):
                    arrived(p, here, o, k)
                    send(p, here, way[hops], o, k, dev)
            else:
                for k in range(2):
                    arrived(p, here, o, k)
                whole.add((p, way[hops], o))
                send(p, here, way[hops], o, None, dev)

    pass_on(0, 0, 0)
    for p in range(2):
        whole.add((p, 0, 1))
        pltpu.make_async_remote_copy(
            src_ref=px.at[p], dst_ref=gath.at[p, 0, 1],
            send_sem=x_send, recv_sem=ag_recv.at[p, 0, 1, 0], device_id=across, device_id_type=MESH,
        ).start()
    pass_on(0, 0, 1)
    for i in range(PIECES):
        loads[n_small + i].wait()
        r = pl.ds(i * piece, piece)
        pltpu.make_async_remote_copy(
            src_ref=g_send.at[r], dst_ref=g_oth.at[r],
            send_sem=gx_send, recv_sem=gx_recv.at[i], device_id=across, device_id_type=MESH,
        ).start()
    for copy in loads[n_small + PIECES :]:
        copy.wait()

    q_at = docs
    x_at = docs + EXTRA
    stages = []

    def exchange(region, c0, c1):
        n = len(stages)
        p, d0, d1, o0, o1 = region
        window, places, sides = pl.ds(c0, c1 - c0), pl.ds(d0, d1 - d0), pl.ds(o0, o1 - o0)
        pltpu.make_async_remote_copy(
            src_ref=part.at[1 - core, p, places, sides, :, window], dst_ref=cx.at[p, places, sides, :, window],
            send_sem=cx_send, recv_sem=cx_recv.at[n], device_id=twin, device_id_type=MESH,
        ).start()
        stages.append((region, c0, c1))

    def multiply(regions, own, x0, x1):
        blocks = []
        for p, d0, d1, o0, o1 in regions:
            for d in range(d0, d1):
                for o in range(o0, o1):
                    for k in range(2):
                        arrived(p, d, o, k)
            blocks.append(gath[p, d0:d1, o0:o1].reshape(-1, keep))
        flat = blocks[0] if len(blocks) == 1 else jnp.concatenate(blocks, axis=0)

        def store(value, c0, c1):
            at = 0
            for p, d0, d1, o0, o1 in regions:
                shape = (d1 - d0, o1 - o0, 2, sub, c1 - c0)
                size = math.prod(shape[:4])
                v = value[at : at + size].reshape(shape)
                at += size
                for k in range(2):
                    part[k, p, d0:d1, o0:o1, :, c0:c1] = v[:, :, k]

        if own:
            store(lax.dot_general(flat, g_own[...], NT, preferred_element_type=F32), 0, docs)
        if x1 > x0:
            weights = g_oth[x0 * piece : x1 * piece]
            dots = lax.dot_general(flat[:, :swap], weights, NT, preferred_element_type=F32)
            store(dots, x_at + x0 * piece, x_at + x1 * piece)
        if own:
            for p, d0, d1, o0, o1 in regions:
                for d in range(d0, d1):
                    for o in range(o0, o1):
                        for k in range(2):
                            v = gath[p, d, o, k].astype(F32)
                            if o == 1:
                                v = v[:, :swap]
                            sq = jnp.sum(v * v, axis=1, keepdims=True)
                            part[k, p, d, o, :, q_at:x_at] = jnp.broadcast_to(sq, (sub, EXTRA))
        fresh[0] = len(stages)
        for region in regions:
            exchange(region, 0 if own else x_at + x0 * piece, x_at + x1 * piece)

    done, fresh = [0], [0]

    def reduce_out(last=False):
        while done[0] < (len(stages) if last else fresh[0]):
            n = done[0]
            done[0] += 1
            (p, d0, d1, o0, o1), c0, c1 = stages[n]
            window, places, sides = pl.ds(c0, c1 - c0), pl.ds(d0, d1 - d0), pl.ds(o0, o1 - o0)
            wait_for(cx.at[p, places, sides, :, window], cx_recv.at[n])
            parts = ((o0, o1),) if p == 0 or o1 - o0 == 1 else ((0, 1), (1, 2))
            for d, (s0, s1) in [(d, side) for d in range(d0, d1) for side in parts]:
                u0, u1 = 2 * p + s0, 2 * p + s1
                units = pl.ds(u0, u1 - u0)
                late = 1 if u1 == 4 else 0
                v = part[core, p, d, s0:s1, :, c0:c1] + cx[p, d, s0:s1, :, c0:c1]
                if c0 <= q_at < c1:
                    sq = v[..., q_at - c0 : x_at - c0]
                    high = sq.astype(BF16).astype(F32)
                    low = (sq - high).astype(BF16).astype(F32)
                    lane = lax.broadcasted_iota(jnp.int32, sq.shape, 2)
                    rs_out[d, u0:u1, :, q_at:x_at] = jnp.where(lane < EXTRA // 2, high, low).astype(BF16)
                    rs_out[d, u0:u1, :, c0:q_at] = v[..., : q_at - c0].astype(BF16)
                    if c1 > x_at:
                        rs_out[d, u0:u1, :, x_at:c1] = v[..., x_at - c0 :].astype(BF16)
                else:
                    rs_out[d, u0:u1, :, c0:c1] = v.astype(BF16)
                owner = lax.rem(z + (OFFSETS[d] + n_z), n_z)

                @pl.when(owner != y)
                def _(d=d, units=units, late=late):
                    pltpu.make_async_remote_copy(
                        src_ref=rs_out.at[d, units, :, window], dst_ref=rs_in.at[y, units, :, window],
                        send_sem=rs_send, recv_sem=rs_recv.at[late],
                        device_id=chip_dev(x_hi * n_y + owner), device_id_type=MESH,
                    ).start()

                @pl.when(owner == y)
                def _(d=d, u0=u0, u1=u1):
                    rs_in[y, u0:u1, :, c0:c1] = rs_out[d, u0:u1, :, c0:c1]

    def doc_squares():
        step = 64
        sums = []
        for i in range(docs // step):
            r = slice(i * step, (i + 1) * step)
            acc = jnp.zeros((step, 128), F32)
            for ref in (g_own, g_send):
                for k in range(ref.shape[1] // 128):
                    v = ref[r, k * 128 : (k + 1) * 128].astype(F32)
                    acc = acc + v * v
            sums.append(acc)
        lanes = jnp.concatenate(sums, axis=0)
        ones = jnp.ones((8, 128), F32)
        sq = lax.dot_general(ones, lanes, NT, preferred_element_type=F32, precision=lax.Precision.HIGHEST)
        ds_part[...] = sq[0:1]
        pltpu.make_async_remote_copy(
            src_ref=ds_part, dst_ref=ds_cx, send_sem=dsc_send, recv_sem=dsc_recv, device_id=twin, device_id_type=MESH
        ).start()

    def doc_spread():
        wait_for(ds_cx, dsc_recv)
        ds_out[...] = ds_part[...] + ds_cx[...]
        ds_in[chip] = ds_out[...]

        def spread(k, carry):
            pltpu.make_async_remote_copy(
                src_ref=ds_out, dst_ref=ds_in.at[chip], send_sem=ds_send, recv_sem=ds_recv,
                device_id=chip_dev(lax.rem(chip + k, chips)), device_id_type=MESH,
            ).start()
            return carry

        lax.fori_loop(1, chips, spread, 0)

    def piece_here(i):
        r = pl.ds(i * piece, piece)
        wait_for(g_oth.at[r], gx_recv.at[i])

    def sum_along_y(o, p):
        acc = rs_in[0, 2 * p + o].astype(F32)
        for k in range(1, n_y):
            acc = acc + rs_in[k, 2 * p + o].astype(F32)
        total[o, p * sub : (p + 1) * sub] = acc

    span = docs + EXTRA

    def send_along_x(o, r0, r1):
        r = pl.ds(r0, r1 - r0)
        owner_hi = lax.rem(col + o, 2)
        other = lax.rem(owner_hi + x_hi, 2)
        row_dev = 2 * (owner_hi * n_y + y) + core
        pltpu.make_async_remote_copy(
            src_ref=total.at[o, r, pl.ds(q_at, span)], dst_ref=fx.at[2 * other, r],
            send_sem=fx_send, recv_sem=fx_recv.at[2 * other],
            device_id=(doc_at(1 - col, 0), row_dev), device_id_type=MESH,
        ).start()

        @pl.when(owner_hi != x_hi)
        def _():
            pltpu.make_async_remote_copy(
                src_ref=total.at[o, r, pl.ds(0, span)], dst_ref=fx.at[1, r],
                send_sem=fx_send, recv_sem=fx_recv.at[1],
                device_id=(doc, row_dev), device_id_type=MESH,
            ).start()

    doc_squares()
    pass_on(1, 0, 0)
    pass_on(0, 1, 0)
    pass_on(0, 1, 1)
    multiply([(0, 0, 1, 0, 2), (0, 1, 3, 0, 1), (1, 0, 1, 0, 2), (1, 1, 3, 0, 1)], True, 0, 0)
    doc_spread()
    pass_on(1, 1, 0)
    reduce_out(last=True)
    pass_on(0, 2, 0)
    pass_on(1, 0, 1)
    multiply([(0, 1, 3, 1, 2), (0, 3, 5, 0, 2)], True, 0, 0)
    piece_here(0)
    multiply([(0, 0, 5, 0, 2), (1, 0, 1, 0, 2), (1, 1, 3, 0, 1)], False, 0, 1)
    reduce_out()
    pass_on(0, 2, 1)
    pass_on(1, 2, 0)
    reduce_out(last=True)
    pass_on(0, 3, 0)
    multiply([(1, 3, 5, 0, 1), (0, 5, 7, 0, 1)], True, 0, 1)
    piece_here(1)
    multiply([(0, 0, 5, 0, 2), (0, 5, 7, 0, 1), (1, 0, 1, 0, 2), (1, 1, 5, 0, 1)], False, 1, 2)
    reduce_out()
    pass_on(1, 1, 1)
    reduce_out(last=True)
    pass_on(0, 3, 1)
    multiply([(1, 1, 3, 1, 2), (1, 5, 7, 0, 1)], True, 0, 2)
    pass_on(1, 3, 0)
    reduce_out(last=True)
    multiply([(0, 5, 7, 1, 2), (0, 7, 8, 0, 1)], True, 0, 2)
    piece_here(2)
    multiply([(0, 0, 7, 0, 2), (0, 7, 8, 0, 1), (1, 0, 3, 0, 2), (1, 3, 7, 0, 1)], False, 2, 3)
    reduce_out()
    pass_on(1, 2, 1, split=True)
    reduce_out(last=True)
    multiply([(1, 3, 5, 1, 2), (1, 7, 8, 0, 1), (0, 7, 8, 1, 2)], True, 0, 3)
    piece_here(3)
    multiply([(0, 0, 8, 0, 2), (1, 0, 5, 0, 2), (1, 5, 8, 0, 1)], False, 3, 4)
    pass_on(1, 3, 1)
    reduce_out()
    multiply([(1, 5, 7, 1, 2)], True, 0, 4)
    reduce_out()
    multiply([(1, 7, 8, 1, 2)], True, 0, 4)
    reduce_out(last=True)

    wait_for(rs_in.at[pl.ds(0, n_y - 1), pl.ds(0, 3)], rs_recv.at[0])
    sum_along_y(0, 0)
    sum_along_y(0, 1)
    sum_along_y(1, 0)
    send_along_x(0, 0, 2 * sub)
    send_along_x(1, 0, sub)
    wait_for(ds_in.at[pl.ds(0, chips - 1)], ds_recv)
    doc_total = jnp.sum(ds_in[...], axis=0)
    wait_for(rs_in.at[pl.ds(0, n_y - 1), 3], rs_recv.at[1])
    sum_along_y(1, 1)
    send_along_x(1, sub, 2 * sub)
    here = total[lax.rem(x_hi + col, 2), :, 0:span]
    for i in range(3):
        wait_for(fx.at[i], fx_recv.at[i])
    dots = here[:, :docs] + fx[1, :, :docs] + fx[0, :, EXTRA:] + fx[2, :, EXTRA:]
    sq = here[:, docs:] + fx[1, :, docs:] + fx[0, :, :EXTRA] + fx[2, :, :EXTRA]
    query_sq = sq[:, 0:1] + sq[:, EXTRA // 2 : EXTRA // 2 + 1]
    out_ref[...] = factor * dots * lax.rsqrt(query_sq + 1e-06) * lax.rsqrt(doc_total + 1e-06)

    wait_for(gath.at[:, pl.ds(0, 7)], ag_send)
    wait_for(px, x_send)
    wait_for(g_oth, gx_send)
    wait_for(cx, cx_send)
    wait_for(rs_out.at[pl.ds(0, n_y - 1)], rs_send)
    wait_for(fx, fx_send)
    wait_for(ds_cx, dsc_send)
    wait_for(ds_in.at[pl.ds(0, chips - 1)], ds_send)


def shards(grads, queries, precond):
    n_doc = lax.axis_size("doc")
    n_layer = lax.axis_size("layer")
    docs, width = grads.shape[0], grads.shape[2]
    rows = queries.shape[0]
    chips = n_layer // 2
    n_y = chips // 2
    own_rows = rows * n_doc // n_layer
    swap = width * 7 // 16
    keep = width - swap
    sub = rows // 4
    places = len(OFFSETS)
    wide = 2 * docs + EXTRA
    factor = math.sqrt(n_layer * width)
    dma = pltpu.SemaphoreType.DMA
    return pl.pallas_call(
        functools.partial(kernel, n_doc, n_layer, swap, factor),
        out_shape=jax.ShapeDtypeStruct((own_rows, docs), F32),
        in_specs=[pl.BlockSpec(memory_space=pltpu.HBM)] * 3,
        out_specs=pl.BlockSpec(memory_space=pltpu.VMEM),
        scratch_shapes=[
            pltpu.VMEM((docs, keep), BF16),
            pltpu.VMEM((docs, swap), BF16),
            pltpu.VMEM((docs, swap), BF16),
            pltpu.VMEM((rows, keep), BF16),
            pltpu.VMEM((rows, swap), BF16),
            pltpu.VMEM((1, keep), F32),
            pltpu.VMEM((1, swap), F32),
            pltpu.VMEM((2, places, 2, 2, sub, keep), BF16),
            pltpu.VMEM((2, 2, sub, keep), BF16),
            pltpu.VMEM((2, 2, places, 2, sub, wide), F32),
            pltpu.VMEM((2, places, 2, sub, wide), F32),
            pltpu.VMEM((places, 4, sub, wide), BF16),
            pltpu.VMEM((n_y, 4, sub, wide), BF16),
            pltpu.VMEM((2, 2 * sub, wide), F32),
            pltpu.VMEM((3, 2 * sub, docs + EXTRA), F32),
            pltpu.VMEM((1, docs), F32),
            pltpu.VMEM((1, docs), F32),
            pltpu.VMEM((1, docs), F32),
            pltpu.VMEM((chips, 1, docs), F32),
            dma((8 + PIECES,)), dma, dma((2, places, 2, 2)), dma, dma, dma((PIECES,)), dma, dma((64,)),
            dma, dma((2,)), dma, dma((3,)), dma, dma, dma, dma,
        ],
        compiler_params=pltpu.CompilerParams(
            collective_id=0, has_side_effects=True, vmem_limit_bytes=48 << 20
        ),
        cost_estimate=pl.CostEstimate(
            flops=2 * rows * n_doc * docs * width, bytes_accessed=2 * docs * width, transcendentals=0
        ),
        name="gather_multiply_reduce",
    )(grads.reshape(docs, width), queries.reshape(rows, width), precond)


def solution(mesh):
    placed = (P("doc", "layer", None), P("doc", "layer", None), P("layer", None))
    return jax.shard_map(
        shards, mesh=mesh, in_specs=placed, out_specs=P("layer", "doc"), check_vma=False
    )
```

```python
import functools
import math

import jax
import jax.numpy as jnp
from jax import lax
from jax.experimental import pallas as pl
from jax.experimental.pallas import tpu as pltpu
from jax.sharding import PartitionSpec as P

MESH = pl.DeviceIdType.MESH
NT = (((1,), (1,)), ((), ()))
F32 = jnp.float32
BF16 = jnp.bfloat16

OFFSETS = (0, -1, 1, -2, 2, -3, 3, 4)
UP = (1, 3, 5, 7)
DOWN = (2, 4, 6, 7)
EXTRA = 128
PIECES = 4


def kernel(
    n_doc, n_layer, swap, factor,
    g_hbm, q_hbm, pc_hbm, out_ref,
    g_own, g_send, g_oth, q_own, q_oth, pc_own, pc_oth, gath, px, part, cx, rs_out, rs_in, total, fx_out, fx,
    ds_part, ds_cx, ds_out, ds_in,
    load, ag_send, ag_recv, x_send, gx_send, gx_recv, cx_send, cx_recv, rs_send, rs_recv, fx_send, fx_recv,
    dsc_send, dsc_recv, ds_send, ds_recv,
):
    n_z = n_doc // 2
    chips = n_layer // 2
    n_y = chips // 2
    docs, keep = g_own.shape
    shared = keep - swap
    rows = q_own.shape[0]
    sub = rows // 4
    piece = docs // PIECES
    doc = lax.axis_index("doc")
    layer = lax.axis_index("layer")
    col = doc // n_z
    z = lax.rem(doc, n_z)
    core = lax.rem(layer, 2)
    chip = layer // 2
    x_hi = chip // n_y
    y = lax.rem(chip, n_y)

    def doc_at(c, dz):
        return c * n_z + lax.rem(z + (dz + n_z), n_z)

    def chip_dev(c):
        return (doc, 2 * c + core)

    up = (doc_at(col, 1), layer)
    down = (doc_at(col, -1), layer)
    across = (doc_at(1 - col, 0), layer)
    twin = (doc, 2 * chip + 1 - core)
    far = (doc_at(1 - col, 0), 2 * ((1 - x_hi) * n_y + y) + core)

    mine = pl.ds(pl.multiple_of(col * swap, 128), swap)
    theirs = pl.ds(pl.multiple_of((1 - col) * swap, 128), swap)
    common = pl.ds(2 * swap, shared)
    first, rest = pl.ds(0, swap), pl.ds(swap, shared)
    loads = [
        (q_hbm.at[:, mine], q_own.at[:, first]),
        (q_hbm.at[:, common], q_own.at[:, rest]),
        (q_hbm.at[:, theirs], q_oth),
        (pc_hbm.at[:, mine], pc_own.at[:, first]),
        (pc_hbm.at[:, common], pc_own.at[:, rest]),
        (pc_hbm.at[:, theirs], pc_oth),
    ]
    n_small = len(loads)
    for i in range(PIECES):
        r = pl.ds(i * piece, piece)
        loads.append((g_hbm.at[r, theirs], g_send.at[r]))
    loads.append((g_hbm.at[:, mine], g_own.at[:, first]))
    loads.append((g_hbm.at[:, common], g_own.at[:, rest]))
    loads = [pltpu.make_async_copy(src, dst, load.at[i]) for i, (src, dst) in enumerate(loads)]
    for copy in loads[:n_small]:
        copy.start()

    barrier = pltpu.get_barrier_semaphore()
    for dev in (up, down, across, twin, far):
        pl.semaphore_signal(barrier, inc=1, device_id=dev, device_id_type=MESH)

    def greet(k, carry):
        pl.semaphore_signal(barrier, inc=1, device_id=chip_dev(lax.rem(chip + k, chips)), device_id_type=MESH)
        return carry

    lax.fori_loop(1, chips, greet, 0)

    for copy in loads[n_small:]:
        copy.start()
    for copy in loads[:n_small]:
        copy.wait()
    pre_own = (q_own[...].astype(F32) * pc_own[...]).astype(BF16)
    pre_oth = (q_oth[...].astype(F32) * pc_oth[...]).astype(BF16)
    for p in range(2):
        for k in range(2):
            r = slice((2 * k + p) * sub, (2 * k + p + 1) * sub)
            gath[p, 0, 0, k] = pre_own[r]
            px[p, k, :, :swap] = pre_oth[r]
            px[p, k, :, swap:] = pre_own[r, swap:]
    pl.semaphore_wait(barrier, 5 + chips - 1)

    def wait_for(ref, sem):
        pltpu.make_async_copy(ref, ref, sem).wait()

    seen = set()
    whole = set()

    def block(p, place, o, k=None):
        return gath.at[p, place, o] if k is None else gath.at[p, place, o, k]

    def send(p, src, dst, o, k, dev):
        pltpu.make_async_remote_copy(
            src_ref=block(p, src, o, k), dst_ref=block(p, dst, o, k),
            send_sem=ag_send, recv_sem=ag_recv.at[p, dst, o, k or 0], device_id=dev, device_id_type=MESH,
        ).start()

    def arrived(p, place, o, k):
        k = None if (p, place, o) in whole else k
        if (p, place, o, k) not in seen and (place, o) != (0, 0):
            seen.add((p, place, o, k))
            wait_for(block(p, place, o, k), ag_recv.at[p, place, o, k or 0])

    def pass_on(o, hops, p, split=False):
        for dev, way, first in ((up, UP, 0), (down, DOWN, 1)):
            here = way[hops - 1] if hops else 0
            if hops == 3 or split:
                for k in (first, 1 - first) if hops < 3 else (first,):
                    arrived(p, here, o, k)
                    send(p, here, way[hops], o, k, dev)
            else:
                for k in range(2):
                    arrived(p, here, o, k)
                whole.add((p, way[hops], o))
                send(p, here, way[hops], o, None, dev)

    pass_on(0, 0, 0)
    for p in range(2):
        whole.add((p, 0, 1))
        pltpu.make_async_remote_copy(
            src_ref=px.at[p], dst_ref=gath.at[p, 0, 1],
            send_sem=x_send, recv_sem=ag_recv.at[p, 0, 1, 0], device_id=across, device_id_type=MESH,
        ).start()
    pass_on(0, 0, 1)
    for i in range(PIECES):
        loads[n_small + i].wait()
        r = pl.ds(i * piece, piece)
        pltpu.make_async_remote_copy(
            src_ref=g_send.at[r], dst_ref=g_oth.at[r],
            send_sem=gx_send, recv_sem=gx_recv.at[i], device_id=across, device_id_type=MESH,
        ).start()
    for copy in loads[n_small + PIECES :]:
        copy.wait()

    q_at = docs
    x_at = docs + EXTRA
    batches = []
    count = [0]

    def exchange(region, c0, c1):
        n = count[0]
        count[0] += 1
        p, d0, d1, o0, o1 = region
        window, places, sides = pl.ds(c0, c1 - c0), pl.ds(d0, d1 - d0), pl.ds(o0, o1 - o0)
        pltpu.make_async_remote_copy(
            src_ref=part.at[1 - core, p, places, sides, :, window], dst_ref=cx.at[p, places, sides, :, window],
            send_sem=cx_send, recv_sem=cx_recv.at[n], device_id=twin, device_id_type=MESH,
        ).start()
        batches[-1].append((n, region, c0, c1))

    def multiply(regions, own, x0, x1):
        blocks = []
        for p, d0, d1, o0, o1 in regions:
            for d in range(d0, d1):
                for o in range(o0, o1):
                    for k in range(2):
                        arrived(p, d, o, k)
            blocks.append(gath[p, d0:d1, o0:o1].reshape(-1, keep))
        flat = blocks[0] if len(blocks) == 1 else jnp.concatenate(blocks, axis=0)

        def store(value, c0, c1):
            at = 0
            for p, d0, d1, o0, o1 in regions:
                shape = (d1 - d0, o1 - o0, 2, sub, c1 - c0)
                size = math.prod(shape[:4])
                v = value[at : at + size].reshape(shape)
                at += size
                for k in range(2):
                    part[k, p, d0:d1, o0:o1, :, c0:c1] = v[:, :, k]

        if own:
            store(lax.dot_general(flat, g_own[...], NT, preferred_element_type=F32), 0, docs)
        if x1 > x0:
            weights = g_oth[x0 * piece : x1 * piece]
            dots = lax.dot_general(flat[:, :swap], weights, NT, preferred_element_type=F32)
            store(dots, x_at + x0 * piece, x_at + x1 * piece)
        if own:
            for p, d0, d1, o0, o1 in regions:
                for d in range(d0, d1):
                    for o in range(o0, o1):
                        for k in range(2):
                            v = gath[p, d, o, k].astype(F32)
                            if o == 1:
                                v = v[:, :swap]
                            sq = jnp.sum(v * v, axis=1, keepdims=True)
                            part[k, p, d, o, :, q_at:x_at] = jnp.broadcast_to(sq, (sub, EXTRA))
        batches.append([])
        for region in regions:
            exchange(region, 0 if own else x_at + x0 * piece, x_at + x1 * piece)

    done = [0]

    def high_low(sq):
        high = sq.astype(BF16).astype(F32)
        low = (sq - high).astype(BF16).astype(F32)
        lane = lax.broadcasted_iota(jnp.int32, sq.shape, sq.ndim - 1)
        return jnp.where(lane < EXTRA // 2, high, low).astype(BF16)

    def reduce_batch(batch):
        units_of = {}
        for n, (p, d0, d1, o0, o1), c0, c1 in batch:
            window, places, sides = pl.ds(c0, c1 - c0), pl.ds(d0, d1 - d0), pl.ds(o0, o1 - o0)
            wait_for(cx.at[p, places, sides, :, window], cx_recv.at[n])
            u0, u1 = 2 * p + o0, 2 * p + o1
            v = part[core, p, d0:d1, o0:o1, :, c0:c1] + cx[p, d0:d1, o0:o1, :, c0:c1]
            if c0 == 0:
                rs_out[d0:d1, u0:u1, :, 0:q_at] = v[..., :q_at].astype(BF16)
                rs_out[d0:d1, u0:u1, :, q_at:x_at] = high_low(v[..., q_at:x_at])
                if c1 > x_at:
                    rs_out[d0:d1, u0:u1, :, x_at:c1] = v[..., x_at:].astype(BF16)
            else:
                rs_out[d0:d1, u0:u1, :, c0:c1] = v.astype(BF16)
            for d in range(d0, d1):
                units_of.setdefault(d, []).append((u0, u1))
        window = pl.ds(c0, c1 - c0)
        for d in sorted(units_of, key=lambda d: -d):
            runs = []
            for u0, u1 in sorted(units_of[d]):
                if runs and runs[-1][1] == u0:
                    runs[-1] = (runs[-1][0], u1)
                else:
                    runs.append((u0, u1))
            owner = lax.rem(z + (OFFSETS[d] + n_z), n_z)

            @pl.when(owner != y)
            def _(d=d, runs=runs, owner=owner):
                for u0, u1 in runs:
                    units = pl.ds(u0, u1 - u0)
                    pltpu.make_async_remote_copy(
                        src_ref=rs_out.at[d, units, :, window], dst_ref=rs_in.at[y, units, :, window],
                        send_sem=rs_send, recv_sem=rs_recv,
                        device_id=chip_dev(x_hi * n_y + owner), device_id_type=MESH,
                    ).start()

            @pl.when(owner == y)
            def _(d=d, runs=runs):
                for u0, u1 in runs:
                    rs_in[y, u0:u1, :, c0:c1] = rs_out[d, u0:u1, :, c0:c1]

    def reduce_out(last=False):
        while done[0] < len(batches) - (0 if last else 1):
            reduce_batch(batches[done[0]])
            done[0] += 1

    def doc_squares():
        step = 64
        sums = []
        for i in range(docs // step):
            r = slice(i * step, (i + 1) * step)
            acc = jnp.zeros((step, 128), F32)
            for ref in (g_own, g_send):
                for k in range(ref.shape[1] // 128):
                    v = ref[r, k * 128 : (k + 1) * 128].astype(F32)
                    acc = acc + v * v
            sums.append(acc)
        lanes = jnp.concatenate(sums, axis=0)
        ones = jnp.ones((8, 128), F32)
        sq = lax.dot_general(ones, lanes, NT, preferred_element_type=F32, precision=lax.Precision.HIGHEST)
        ds_part[...] = sq[0:1]
        pltpu.make_async_remote_copy(
            src_ref=ds_part, dst_ref=ds_cx, send_sem=dsc_send, recv_sem=dsc_recv, device_id=twin, device_id_type=MESH
        ).start()

    def doc_spread():
        wait_for(ds_cx, dsc_recv)
        ds_out[...] = ds_part[...] + ds_cx[...]
        ds_in[chip] = ds_out[...]

        def spread(k, carry):
            pltpu.make_async_remote_copy(
                src_ref=ds_out, dst_ref=ds_in.at[chip], send_sem=ds_send, recv_sem=ds_recv,
                device_id=chip_dev(lax.rem(chip + k, chips)), device_id_type=MESH,
            ).start()
            return carry

        lax.fori_loop(1, chips, spread, 0)

    def piece_here(i):
        r = pl.ds(i * piece, piece)
        wait_for(g_oth.at[r], gx_recv.at[i])

    def sum_along_y(o, p):
        acc = rs_in[0, 2 * p + o].astype(F32)
        for k in range(1, n_y):
            acc = acc + rs_in[k, 2 * p + o].astype(F32)
        total[o, p * sub : (p + 1) * sub] = acc

    span = docs + EXTRA

    def send_along_x(o):
        v = total[o]
        sq = v[:, q_at : q_at + 1] + v[:, q_at + EXTRA // 2 : q_at + EXTRA // 2 + 1]
        fx_out[o, :, 0:q_at] = v[:, 0:q_at].astype(BF16)
        fx_out[o, :, q_at:x_at] = high_low(jnp.broadcast_to(sq, (2 * sub, EXTRA)))
        fx_out[o, :, x_at:] = v[:, x_at:].astype(BF16)
        owner_hi = lax.rem(col + o, 2)
        other = lax.rem(owner_hi + x_hi, 2)
        row_dev = 2 * (owner_hi * n_y + y) + core
        pltpu.make_async_remote_copy(
            src_ref=fx_out.at[o, :, pl.ds(q_at, span)], dst_ref=fx.at[2 * other],
            send_sem=fx_send, recv_sem=fx_recv.at[2 * other],
            device_id=(doc_at(1 - col, 0), row_dev), device_id_type=MESH,
        ).start()

        @pl.when(owner_hi != x_hi)
        def _():
            pltpu.make_async_remote_copy(
                src_ref=fx_out.at[o, :, pl.ds(0, span)], dst_ref=fx.at[1],
                send_sem=fx_send, recv_sem=fx_recv.at[1],
                device_id=(doc, row_dev), device_id_type=MESH,
            ).start()

    doc_squares()
    pass_on(0, 1, 0)
    pass_on(1, 0, 0)
    multiply([(0, 0, 1, 0, 2), (0, 1, 3, 0, 1), (1, 0, 1, 0, 2), (1, 1, 3, 0, 1)], True, 0, 0)
    doc_spread()
    pass_on(0, 2, 0)
    reduce_out(last=True)
    pass_on(1, 1, 0)
    multiply([(0, 3, 5, 0, 1), (0, 1, 3, 1, 2)], True, 0, 0)
    piece_here(0)
    multiply([(0, 0, 3, 0, 2), (0, 3, 5, 0, 1), (1, 0, 1, 0, 2), (1, 1, 3, 0, 1)], False, 0, 1)
    pass_on(0, 3, 0)
    reduce_out()
    pass_on(1, 2, 0)
    pass_on(0, 1, 1)
    reduce_out(last=True)
    multiply([(0, 5, 8, 0, 1), (0, 3, 5, 1, 2)], True, 0, 1)
    piece_here(1)
    multiply([(0, 0, 5, 0, 2), (0, 5, 8, 0, 1), (1, 0, 1, 0, 2), (1, 1, 3, 0, 1)], False, 1, 2)
    pass_on(1, 3, 0)
    pass_on(1, 0, 1)
    reduce_out()
    pass_on(0, 2, 1)
    reduce_out(last=True)
    multiply([(0, 5, 8, 1, 2), (1, 3, 5, 0, 1)], True, 0, 2)
    pass_on(1, 1, 1)
    reduce_out(last=True)
    piece_here(2)
    multiply([(0, 0, 8, 0, 2), (1, 0, 1, 0, 2), (1, 1, 5, 0, 1)], False, 2, 3)
    pass_on(0, 3, 1)
    reduce_out()
    multiply([(1, 1, 3, 1, 2), (1, 5, 7, 0, 1)], True, 0, 3)
    pass_on(1, 2, 1, split=True)
    reduce_out(last=True)
    multiply([(1, 3, 5, 1, 2), (1, 7, 8, 0, 1)], True, 0, 3)
    reduce_out()
    pass_on(1, 3, 1)
    piece_here(3)
    multiply([(0, 0, 8, 0, 2), (1, 0, 5, 0, 2), (1, 5, 8, 0, 1)], False, 3, 4)
    reduce_out(last=True)
    multiply([(1, 5, 7, 1, 2)], True, 0, 4)
    reduce_out(last=True)
    multiply([(1, 7, 8, 1, 2)], True, 0, 4)
    reduce_out(last=True)

    wait_for(rs_in.at[pl.ds(0, n_y - 1)], rs_recv)
    for o in range(2):
        for p in range(2):
            sum_along_y(o, p)
        send_along_x(o)
    wait_for(ds_in.at[pl.ds(0, chips - 1)], ds_recv)
    doc_total = jnp.sum(ds_in[...], axis=0)
    here = total[lax.rem(x_hi + col, 2), :, 0:span]
    for i in range(3):
        wait_for(fx.at[i], fx_recv.at[i])
    got = [fx[i].astype(F32) for i in range(3)]
    dots = here[:, :docs] + got[1][:, :docs] + got[0][:, EXTRA:] + got[2][:, EXTRA:]
    sq = here[:, docs:] + got[1][:, docs:] + got[0][:, :EXTRA] + got[2][:, :EXTRA]
    query_sq = sq[:, 0:1] + sq[:, EXTRA // 2 : EXTRA // 2 + 1]
    out_ref[...] = factor * dots * lax.rsqrt(query_sq + 1e-06) * lax.rsqrt(doc_total + 1e-06)

    wait_for(gath.at[:, pl.ds(0, 7)], ag_send)
    wait_for(px, x_send)
    wait_for(g_oth, gx_send)
    wait_for(cx, cx_send)
    wait_for(rs_out.at[pl.ds(0, n_y - 1)], rs_send)
    wait_for(fx, fx_send)
    wait_for(ds_cx, dsc_send)
    wait_for(ds_in.at[pl.ds(0, chips - 1)], ds_send)


def shards(grads, queries, precond):
    n_doc = lax.axis_size("doc")
    n_layer = lax.axis_size("layer")
    docs, width = grads.shape[0], grads.shape[2]
    rows = queries.shape[0]
    chips = n_layer // 2
    n_y = chips // 2
    own_rows = rows * n_doc // n_layer
    swap = width * 13 // 32
    keep = width - swap
    sub = rows // 4
    places = len(OFFSETS)
    wide = 2 * docs + EXTRA
    factor = math.sqrt(n_layer * width)
    dma = pltpu.SemaphoreType.DMA
    return pl.pallas_call(
        functools.partial(kernel, n_doc, n_layer, swap, factor),
        out_shape=jax.ShapeDtypeStruct((own_rows, docs), F32),
        in_specs=[pl.BlockSpec(memory_space=pltpu.HBM)] * 3,
        out_specs=pl.BlockSpec(memory_space=pltpu.VMEM),
        scratch_shapes=[
            pltpu.VMEM((docs, keep), BF16),
            pltpu.VMEM((docs, swap), BF16),
            pltpu.VMEM((docs, swap), BF16),
            pltpu.VMEM((rows, keep), BF16),
            pltpu.VMEM((rows, swap), BF16),
            pltpu.VMEM((1, keep), F32),
            pltpu.VMEM((1, swap), F32),
            pltpu.VMEM((2, places, 2, 2, sub, keep), BF16),
            pltpu.VMEM((2, 2, sub, keep), BF16),
            pltpu.VMEM((2, 2, places, 2, sub, wide), F32),
            pltpu.VMEM((2, places, 2, sub, wide), F32),
            pltpu.VMEM((places, 4, sub, wide), BF16),
            pltpu.VMEM((n_y, 4, sub, wide), BF16),
            pltpu.VMEM((2, 2 * sub, wide), F32),
            pltpu.VMEM((2, 2 * sub, wide), BF16),
            pltpu.VMEM((3, 2 * sub, docs + EXTRA), BF16),
            pltpu.VMEM((1, docs), F32),
            pltpu.VMEM((1, docs), F32),
            pltpu.VMEM((1, docs), F32),
            pltpu.VMEM((chips, 1, docs), F32),
            dma((8 + PIECES,)), dma, dma((2, places, 2, 2)), dma, dma, dma((PIECES,)), dma, dma((64,)),
            dma, dma, dma, dma((3,)), dma, dma, dma, dma,
        ],
        compiler_params=pltpu.CompilerParams(
            collective_id=0, has_side_effects=True, vmem_limit_bytes=63 << 20
        ),
        cost_estimate=pl.CostEstimate(
            flops=2 * rows * n_doc * docs * width, bytes_accessed=2 * docs * width, transcendentals=0
        ),
        name="gather_multiply_reduce",
    )(grads.reshape(docs, width), queries.reshape(rows, width), precond)


def solution(mesh):
    placed = (P("doc", "layer", None), P("doc", "layer", None), P("layer", None))
    return jax.shard_map(
        shards, mesh=mesh, in_specs=placed, out_specs=P("layer", "doc"), check_vma=False
    )
```

```python
import functools
import math

import jax
import jax.numpy as jnp
from jax import lax
from jax.experimental import pallas as pl
from jax.experimental.pallas import tpu as pltpu
from jax.sharding import PartitionSpec as P

MESH = pl.DeviceIdType.MESH
NT = (((1,), (1,)), ((), ()))
F32 = jnp.float32
BF16 = jnp.bfloat16

OFFSETS = (0, -1, 1, -2, 2, -3, 3, 4)
UP = (1, 3, 5, 7)
DOWN = (2, 4, 6, 7)
FAR = ((1, 5, 7, 1, 2), (1, 7, 8, 1, 2))
EXTRA = 128
PIECES = 4


def kernel(
    n_doc, n_layer, swap, factor,
    g_hbm, q_hbm, pc_hbm, out_ref,
    g_own, g_send, g_oth, q_own, q_oth, pc_own, pc_oth, gath, px, part, cx, rs_out, rs_in, total, fx_out, fx,
    ds_part, ds_cx, ds_out, ds_in,
    load, ag_send, ag_recv, x_send, gx_send, gx_recv, cx_send, cx_recv, rs_send, rs_recv, fx_send, fx_recv,
    dsc_send, dsc_recv, ds_send, ds_recv,
):
    n_z = n_doc // 2
    chips = n_layer // 2
    n_y = chips // 2
    docs, keep = g_own.shape
    shared = keep - swap
    rows = q_own.shape[0]
    sub = rows // 4
    piece = docs // PIECES
    doc = lax.axis_index("doc")
    layer = lax.axis_index("layer")
    col = doc // n_z
    z = lax.rem(doc, n_z)
    core = lax.rem(layer, 2)
    chip = layer // 2
    x_hi = chip // n_y
    y = lax.rem(chip, n_y)

    def doc_at(c, dz):
        return c * n_z + lax.rem(z + (dz + n_z), n_z)

    def chip_dev(c):
        return (doc, 2 * c + core)

    up = (doc_at(col, 1), layer)
    down = (doc_at(col, -1), layer)
    across = (doc_at(1 - col, 0), layer)
    twin = (doc, 2 * chip + 1 - core)
    far = (doc_at(1 - col, 0), 2 * ((1 - x_hi) * n_y + y) + core)

    mine = pl.ds(pl.multiple_of(col * swap, 128), swap)
    theirs = pl.ds(pl.multiple_of((1 - col) * swap, 128), swap)
    common = pl.ds(2 * swap, shared)
    first, rest = pl.ds(0, swap), pl.ds(swap, shared)
    loads = [
        (q_hbm.at[:, mine], q_own.at[:, first]),
        (q_hbm.at[:, common], q_own.at[:, rest]),
        (q_hbm.at[:, theirs], q_oth),
        (pc_hbm.at[:, mine], pc_own.at[:, first]),
        (pc_hbm.at[:, common], pc_own.at[:, rest]),
        (pc_hbm.at[:, theirs], pc_oth),
    ]
    n_small = len(loads)
    for i in range(PIECES):
        r = pl.ds(i * piece, piece)
        loads.append((g_hbm.at[r, theirs], g_send.at[r]))
    loads.append((g_hbm.at[:, mine], g_own.at[:, first]))
    loads.append((g_hbm.at[:, common], g_own.at[:, rest]))
    loads = [pltpu.make_async_copy(src, dst, load.at[i]) for i, (src, dst) in enumerate(loads)]
    for copy in loads[:n_small]:
        copy.start()

    barrier = pltpu.get_barrier_semaphore()
    for dev in (up, down, across, twin, far):
        pl.semaphore_signal(barrier, inc=1, device_id=dev, device_id_type=MESH)

    def greet(k, carry):
        pl.semaphore_signal(barrier, inc=1, device_id=chip_dev(lax.rem(chip + k, chips)), device_id_type=MESH)
        return carry

    lax.fori_loop(1, chips, greet, 0)

    for copy in loads[n_small:]:
        copy.start()
    for copy in loads[:n_small]:
        copy.wait()
    shared_at = pl.ds(swap, shared)

    def weigh(p):
        for k in range(2):
            r = pl.ds((2 * k + p) * sub, sub)
            gath[p, 0, 0, k] = (q_own[r, :].astype(F32) * pc_own[...]).astype(BF16)
            px[p, k, :, 0:swap] = (q_oth[r, :].astype(F32) * pc_oth[...]).astype(BF16)
            px[p, k, :, shared_at] = gath[p, 0, 0, k, :, shared_at]

    weigh(0)
    pl.semaphore_wait(barrier, 5 + chips - 1)

    def wait_for(ref, sem):
        pltpu.make_async_copy(ref, ref, sem).wait()

    seen = set()
    whole = set()

    def block(p, place, o, k=None):
        return gath.at[p, place, o] if k is None else gath.at[p, place, o, k]

    def send(p, src, dst, o, k, dev):
        pltpu.make_async_remote_copy(
            src_ref=block(p, src, o, k), dst_ref=block(p, dst, o, k),
            send_sem=ag_send, recv_sem=ag_recv.at[p, dst, o, k or 0], device_id=dev, device_id_type=MESH,
        ).start()

    def arrived(p, place, o, k):
        k = None if (p, place, o) in whole else k
        if (p, place, o, k) not in seen and (place, o) != (0, 0):
            seen.add((p, place, o, k))
            wait_for(block(p, place, o, k), ag_recv.at[p, place, o, k or 0])

    def pass_on(o, hops, p, split=False):
        for dev, way, first in ((up, UP, 0), (down, DOWN, 1)):
            here = way[hops - 1] if hops else 0
            if hops == 3 or split:
                for k in (first, 1 - first) if hops < 3 else (first,):
                    arrived(p, here, o, k)
                    send(p, here, way[hops], o, k, dev)
            else:
                for k in range(2):
                    arrived(p, here, o, k)
                whole.add((p, way[hops], o))
                send(p, here, way[hops], o, None, dev)

    for p in range(2):
        if p == 1:
            weigh(1)
        pass_on(0, 0, p)
        whole.add((p, 0, 1))
        pltpu.make_async_remote_copy(
            src_ref=px.at[p], dst_ref=gath.at[p, 0, 1],
            send_sem=x_send, recv_sem=ag_recv.at[p, 0, 1, 0], device_id=across, device_id_type=MESH,
        ).start()
    for i in range(PIECES):
        loads[n_small + i].wait()
        r = pl.ds(i * piece, piece)
        pltpu.make_async_remote_copy(
            src_ref=g_send.at[r], dst_ref=g_oth.at[r],
            send_sem=gx_send, recv_sem=gx_recv.at[i], device_id=across, device_id_type=MESH,
        ).start()
    for copy in loads[n_small + PIECES :]:
        copy.wait()

    q_at = docs
    x_at = docs + EXTRA
    batches = []
    count = [0]

    def exchange(region, c0, c1):
        n = count[0]
        count[0] += 1
        p, d0, d1, o0, o1 = region
        window, places, sides = pl.ds(c0, c1 - c0), pl.ds(d0, d1 - d0), pl.ds(o0, o1 - o0)
        pltpu.make_async_remote_copy(
            src_ref=part.at[1 - core, p, places, sides, :, window], dst_ref=cx.at[p, places, sides, :, window],
            send_sem=cx_send, recv_sem=cx_recv.at[n], device_id=twin, device_id_type=MESH,
        ).start()
        batches[-1].append((n, region, c0, c1))

    def multiply(regions, own, x0, x1):
        blocks = []
        for p, d0, d1, o0, o1 in regions:
            for d in range(d0, d1):
                for o in range(o0, o1):
                    for k in range(2):
                        arrived(p, d, o, k)
            blocks.append(gath[p, d0:d1, o0:o1].reshape(-1, keep))
        flat = blocks[0] if len(blocks) == 1 else jnp.concatenate(blocks, axis=0)

        def store(value, c0, c1):
            at = 0
            for p, d0, d1, o0, o1 in regions:
                shape = (d1 - d0, o1 - o0, 2, sub, c1 - c0)
                size = math.prod(shape[:4])
                v = value[at : at + size].reshape(shape)
                at += size
                for k in range(2):
                    part[k, p, d0:d1, o0:o1, :, c0:c1] = v[:, :, k]

        if own:
            store(lax.dot_general(flat, g_own[...], NT, preferred_element_type=F32), 0, docs)
        if x1 > x0:
            weights = g_oth[x0 * piece : x1 * piece]
            dots = lax.dot_general(flat[:, :swap], weights, NT, preferred_element_type=F32)
            store(dots, x_at + x0 * piece, x_at + x1 * piece)
        if own:
            for p, d0, d1, o0, o1 in regions:
                for d in range(d0, d1):
                    for o in range(o0, o1):
                        for k in range(2):
                            v = gath[p, d, o, k].astype(F32)
                            if o == 1:
                                v = v[:, :swap]
                            sq = jnp.sum(v * v, axis=1, keepdims=True)
                            part[k, p, d, o, :, q_at:x_at] = jnp.broadcast_to(sq, (sub, EXTRA))
        batches.append([])
        for region in regions:
            exchange(region, 0 if own else x_at + x0 * piece, x_at + x1 * piece)

    done = [0]

    def high_low(sq):
        high = sq.astype(BF16).astype(F32)
        low = (sq - high).astype(BF16).astype(F32)
        lane = lax.broadcasted_iota(jnp.int32, sq.shape, sq.ndim - 1)
        return jnp.where(lane < EXTRA // 2, high, low).astype(BF16)

    def reduce_batch(batch):
        units_of = {}
        late = 1 if batch[0][1] in FAR else 0
        for n, (p, d0, d1, o0, o1), c0, c1 in batch:
            window, places, sides = pl.ds(c0, c1 - c0), pl.ds(d0, d1 - d0), pl.ds(o0, o1 - o0)
            wait_for(cx.at[p, places, sides, :, window], cx_recv.at[n])
            u0, u1 = 2 * p + o0, 2 * p + o1
            v = part[core, p, d0:d1, o0:o1, :, c0:c1] + cx[p, d0:d1, o0:o1, :, c0:c1]
            if c0 == 0:
                rs_out[d0:d1, u0:u1, :, 0:q_at] = v[..., :q_at].astype(BF16)
                rs_out[d0:d1, u0:u1, :, q_at:x_at] = high_low(v[..., q_at:x_at])
                if c1 > x_at:
                    rs_out[d0:d1, u0:u1, :, x_at:c1] = v[..., x_at:].astype(BF16)
            else:
                rs_out[d0:d1, u0:u1, :, c0:c1] = v.astype(BF16)
            for d in range(d0, d1):
                units_of.setdefault(d, []).append((u0, u1))
        window = pl.ds(c0, c1 - c0)
        for d in sorted(units_of, key=lambda d: -d):
            runs = []
            for u0, u1 in sorted(units_of[d]):
                if runs and runs[-1][1] == u0:
                    runs[-1] = (runs[-1][0], u1)
                else:
                    runs.append((u0, u1))
            owner = lax.rem(z + (OFFSETS[d] + n_z), n_z)

            @pl.when(owner != y)
            def _(d=d, runs=runs, owner=owner):
                for u0, u1 in runs:
                    units = pl.ds(u0, u1 - u0)
                    pltpu.make_async_remote_copy(
                        src_ref=rs_out.at[d, units, :, window], dst_ref=rs_in.at[y, units, :, window],
                        send_sem=rs_send, recv_sem=rs_recv.at[late],
                        device_id=chip_dev(x_hi * n_y + owner), device_id_type=MESH,
                    ).start()

            @pl.when(owner == y)
            def _(d=d, runs=runs):
                for u0, u1 in runs:
                    rs_in[y, u0:u1, :, c0:c1] = rs_out[d, u0:u1, :, c0:c1]

    def reduce_out(last=False):
        while done[0] < len(batches) - (0 if last else 1):
            reduce_batch(batches[done[0]])
            done[0] += 1

    def doc_squares():
        step = 64
        sums = []
        for i in range(docs // step):
            r = slice(i * step, (i + 1) * step)
            acc = jnp.zeros((step, 128), F32)
            for ref in (g_own, g_send):
                for k in range(ref.shape[1] // 128):
                    v = ref[r, k * 128 : (k + 1) * 128].astype(F32)
                    acc = acc + v * v
            sums.append(acc)
        lanes = jnp.concatenate(sums, axis=0)
        ones = jnp.ones((8, 128), F32)
        sq = lax.dot_general(ones, lanes, NT, preferred_element_type=F32, precision=lax.Precision.HIGHEST)
        ds_part[...] = sq[0:1]
        pltpu.make_async_remote_copy(
            src_ref=ds_part, dst_ref=ds_cx, send_sem=dsc_send, recv_sem=dsc_recv, device_id=twin, device_id_type=MESH
        ).start()

    def doc_spread():
        wait_for(ds_cx, dsc_recv)
        ds_out[...] = ds_part[...] + ds_cx[...]
        ds_in[chip] = ds_out[...]

        def spread(k, carry):
            pltpu.make_async_remote_copy(
                src_ref=ds_out, dst_ref=ds_in.at[chip], send_sem=ds_send, recv_sem=ds_recv,
                device_id=chip_dev(lax.rem(chip + k, chips)), device_id_type=MESH,
            ).start()
            return carry

        lax.fori_loop(1, chips, spread, 0)

    def piece_here(i):
        r = pl.ds(i * piece, piece)
        wait_for(g_oth.at[r], gx_recv.at[i])

    def sum_along_y(o, p):
        acc = rs_in[0, 2 * p + o].astype(F32)
        for k in range(1, n_y):
            acc = acc + rs_in[k, 2 * p + o].astype(F32)
        total[o, p * sub : (p + 1) * sub] = acc

    span = docs + EXTRA

    def send_along_x(o):
        v = total[o]
        sq = v[:, q_at : q_at + 1] + v[:, q_at + EXTRA // 2 : q_at + EXTRA // 2 + 1]
        fx_out[o, :, 0:q_at] = v[:, 0:q_at].astype(BF16)
        fx_out[o, :, q_at:x_at] = high_low(jnp.broadcast_to(sq, (2 * sub, EXTRA)))
        fx_out[o, :, x_at:] = v[:, x_at:].astype(BF16)
        owner_hi = lax.rem(col + o, 2)
        other = lax.rem(owner_hi + x_hi, 2)
        row_dev = 2 * (owner_hi * n_y + y) + core
        pltpu.make_async_remote_copy(
            src_ref=fx_out.at[o, :, pl.ds(q_at, span)], dst_ref=fx.at[2 * other],
            send_sem=fx_send, recv_sem=fx_recv.at[2 * other],
            device_id=(doc_at(1 - col, 0), row_dev), device_id_type=MESH,
        ).start()

        @pl.when(owner_hi != x_hi)
        def _():
            pltpu.make_async_remote_copy(
                src_ref=fx_out.at[o, :, pl.ds(0, span)], dst_ref=fx.at[1],
                send_sem=fx_send, recv_sem=fx_recv.at[1],
                device_id=(doc, row_dev), device_id_type=MESH,
            ).start()

    doc_squares()
    pass_on(0, 1, 0)
    pass_on(1, 0, 0)
    multiply([(0, 0, 1, 0, 2), (0, 1, 3, 0, 1), (1, 0, 1, 0, 2), (1, 1, 3, 0, 1)], True, 0, 0)
    doc_spread()
    pass_on(0, 2, 0)
    reduce_out(last=True)
    pass_on(1, 1, 0)
    multiply([(0, 3, 5, 0, 1), (0, 1, 3, 1, 2)], True, 0, 0)
    piece_here(0)
    multiply([(0, 0, 3, 0, 2), (0, 3, 5, 0, 1), (1, 0, 1, 0, 2), (1, 1, 3, 0, 1)], False, 0, 1)
    pass_on(0, 3, 0)
    reduce_out()
    pass_on(1, 2, 0)
    pass_on(0, 1, 1)
    reduce_out(last=True)
    multiply([(0, 5, 8, 0, 1), (0, 3, 5, 1, 2)], True, 0, 1)
    piece_here(1)
    multiply([(0, 0, 5, 0, 2), (0, 5, 8, 0, 1), (1, 0, 1, 0, 2), (1, 1, 3, 0, 1)], False, 1, 2)
    pass_on(1, 3, 0)
    pass_on(1, 0, 1)
    reduce_out()
    pass_on(0, 2, 1)
    reduce_out(last=True)
    multiply([(0, 5, 8, 1, 2), (1, 3, 5, 0, 1)], True, 0, 2)
    pass_on(1, 1, 1)
    reduce_out(last=True)
    piece_here(2)
    multiply([(0, 0, 8, 0, 2), (1, 0, 1, 0, 2), (1, 1, 5, 0, 1)], False, 2, 3)
    pass_on(0, 3, 1)
    reduce_out()
    multiply([(1, 1, 3, 1, 2), (1, 5, 7, 0, 1)], True, 0, 3)
    pass_on(1, 2, 1, split=True)
    reduce_out(last=True)
    multiply([(1, 3, 5, 1, 2), (1, 7, 8, 0, 1)], True, 0, 3)
    reduce_out()
    pass_on(1, 3, 1)
    piece_here(3)
    multiply([(0, 0, 8, 0, 2), (1, 0, 5, 0, 2), (1, 5, 8, 0, 1)], False, 3, 4)
    reduce_out(last=True)
    multiply([FAR[0]], True, 0, 4)
    reduce_out(last=True)
    multiply([FAR[1]], True, 0, 4)
    reduce_out(last=True)

    distance = lax.rem(y - z + 2 * n_y, n_y)
    far = jnp.logical_and(distance >= 3, distance <= n_y - 3)

    @pl.when(far)
    def _():
        wait_for(rs_in.at[pl.ds(0, n_y - 1), pl.ds(0, 3)], rs_recv.at[0])

    @pl.when(jnp.logical_not(far))
    def _():
        wait_for(rs_in.at[pl.ds(0, n_y - 1)], rs_recv.at[0])

    sum_along_y(0, 0)
    sum_along_y(0, 1)
    send_along_x(0)
    sum_along_y(1, 0)

    @pl.when(far)
    def _():
        wait_for(rs_in.at[pl.ds(0, n_y - 1), 3], rs_recv.at[1])

    sum_along_y(1, 1)
    send_along_x(1)
    wait_for(ds_in.at[pl.ds(0, chips - 1)], ds_recv)
    doc_total = jnp.sum(ds_in[...], axis=0)
    here = total[lax.rem(x_hi + col, 2), :, 0:span]
    for i in range(3):
        wait_for(fx.at[i], fx_recv.at[i])
    got = [fx[i].astype(F32) for i in range(3)]
    dots = here[:, :docs] + got[1][:, :docs] + got[0][:, EXTRA:] + got[2][:, EXTRA:]
    sq = here[:, docs:] + got[1][:, docs:] + got[0][:, :EXTRA] + got[2][:, :EXTRA]
    query_sq = sq[:, 0:1] + sq[:, EXTRA // 2 : EXTRA // 2 + 1]
    out_ref[...] = factor * dots * lax.rsqrt(query_sq + 1e-06) * lax.rsqrt(doc_total + 1e-06)

    wait_for(gath.at[:, pl.ds(0, 7)], ag_send)
    wait_for(px, x_send)
    wait_for(g_oth, gx_send)
    wait_for(cx, cx_send)
    wait_for(rs_out.at[pl.ds(0, n_y - 1)], rs_send)
    wait_for(fx, fx_send)
    wait_for(ds_cx, dsc_send)
    wait_for(ds_in.at[pl.ds(0, chips - 1)], ds_send)


def shards(grads, queries, precond):
    n_doc = lax.axis_size("doc")
    n_layer = lax.axis_size("layer")
    docs, width = grads.shape[0], grads.shape[2]
    rows = queries.shape[0]
    chips = n_layer // 2
    n_y = chips // 2
    own_rows = rows * n_doc // n_layer
    swap = width * 13 // 32
    keep = width - swap
    sub = rows // 4
    places = len(OFFSETS)
    wide = 2 * docs + EXTRA
    factor = math.sqrt(n_layer * width)
    dma = pltpu.SemaphoreType.DMA
    return pl.pallas_call(
        functools.partial(kernel, n_doc, n_layer, swap, factor),
        out_shape=jax.ShapeDtypeStruct((own_rows, docs), F32),
        in_specs=[pl.BlockSpec(memory_space=pltpu.HBM)] * 3,
        out_specs=pl.BlockSpec(memory_space=pltpu.VMEM),
        scratch_shapes=[
            pltpu.VMEM((docs, keep), BF16),
            pltpu.VMEM((docs, swap), BF16),
            pltpu.VMEM((docs, swap), BF16),
            pltpu.VMEM((rows, keep), BF16),
            pltpu.VMEM((rows, swap), BF16),
            pltpu.VMEM((1, keep), F32),
            pltpu.VMEM((1, swap), F32),
            pltpu.VMEM((2, places, 2, 2, sub, keep), BF16),
            pltpu.VMEM((2, 2, sub, keep), BF16),
            pltpu.VMEM((2, 2, places, 2, sub, wide), F32),
            pltpu.VMEM((2, places, 2, sub, wide), F32),
            pltpu.VMEM((places, 4, sub, wide), BF16),
            pltpu.VMEM((n_y, 4, sub, wide), BF16),
            pltpu.VMEM((2, 2 * sub, wide), F32),
            pltpu.VMEM((2, 2 * sub, wide), BF16),
            pltpu.VMEM((3, 2 * sub, docs + EXTRA), BF16),
            pltpu.VMEM((1, docs), F32),
            pltpu.VMEM((1, docs), F32),
            pltpu.VMEM((1, docs), F32),
            pltpu.VMEM((chips, 1, docs), F32),
            dma((8 + PIECES,)), dma, dma((2, places, 2, 2)), dma, dma, dma((PIECES,)), dma, dma((64,)),
            dma, dma((2,)), dma, dma((3,)), dma, dma, dma, dma,
        ],
        compiler_params=pltpu.CompilerParams(
            collective_id=0, has_side_effects=True, vmem_limit_bytes=63 << 20
        ),
        cost_estimate=pl.CostEstimate(
            flops=2 * rows * n_doc * docs * width, bytes_accessed=2 * docs * width, transcendentals=0
        ),
        name="gather_multiply_reduce",
    )(grads.reshape(docs, width), queries.reshape(rows, width), precond)


def solution(mesh):
    placed = (P("doc", "layer", None), P("doc", "layer", None), P("layer", None))
    return jax.shard_map(
        shards, mesh=mesh, in_specs=placed, out_specs=P("layer", "doc"), check_vma=False
    )
```

```python
import functools
import math

import jax
import jax.numpy as jnp
from jax import lax
from jax.experimental import pallas as pl
from jax.experimental.pallas import tpu as pltpu
from jax.sharding import PartitionSpec as P

MESH = pl.DeviceIdType.MESH
NT = (((1,), (1,)), ((), ()))
F32 = jnp.float32
BF16 = jnp.bfloat16

OFFSETS = (0, -1, 1, -2, 2, -3, 3, 4)
UP = (1, 3, 5, 7)
DOWN = (2, 4, 6, 7)
FAR = ((1, 5, 7, 1, 2), (1, 7, 8, 1, 2))
EXTRA = 128
PIECES = 4


def kernel(
    n_doc, n_layer, swap, factor,
    g_hbm, q_hbm, pc_hbm, out_ref,
    g_own, g_send, g_oth, q_own, q_oth, pc_own, pc_oth, gath, px, part, cx, rs_out, rs_in, total, fx_out, fx,
    ds_part, ds_cx, ds_out, ds_in,
    load, ag_send, ag_recv, x_send, gx_send, gx_recv, cx_send, cx_recv, rs_send, rs_recv, fx_send, fx_recv,
    dsc_send, dsc_recv, ds_send, ds_recv,
):
    n_z = n_doc // 2
    chips = n_layer // 2
    n_y = chips // 2
    docs, keep = g_own.shape
    shared = keep - swap
    rows = q_own.shape[0]
    sub = rows // 4
    piece = docs // PIECES
    doc = lax.axis_index("doc")
    layer = lax.axis_index("layer")
    col = doc // n_z
    z = lax.rem(doc, n_z)
    core = lax.rem(layer, 2)
    chip = layer // 2
    x_hi = chip // n_y
    y = lax.rem(chip, n_y)

    def doc_at(c, dz):
        return c * n_z + lax.rem(z + (dz + n_z), n_z)

    def chip_dev(c):
        return (doc, 2 * c + core)

    up = (doc_at(col, 1), layer)
    down = (doc_at(col, -1), layer)
    across = (doc_at(1 - col, 0), layer)
    twin = (doc, 2 * chip + 1 - core)
    far = (doc_at(1 - col, 0), 2 * ((1 - x_hi) * n_y + y) + core)

    mine = pl.ds(pl.multiple_of(col * swap, 128), swap)
    theirs = pl.ds(pl.multiple_of((1 - col) * swap, 128), swap)
    common = pl.ds(2 * swap, shared)
    first, rest = pl.ds(0, swap), pl.ds(swap, shared)
    loads = [
        (q_hbm.at[:, mine], q_own.at[:, first]),
        (q_hbm.at[:, common], q_own.at[:, rest]),
        (q_hbm.at[:, theirs], q_oth),
        (pc_hbm.at[:, mine], pc_own.at[:, first]),
        (pc_hbm.at[:, common], pc_own.at[:, rest]),
        (pc_hbm.at[:, theirs], pc_oth),
    ]
    n_small = len(loads)
    for i in range(PIECES):
        r = pl.ds(i * piece, piece)
        loads.append((g_hbm.at[r, theirs], g_send.at[r]))
    loads.append((g_hbm.at[:, mine], g_own.at[:, first]))
    loads.append((g_hbm.at[:, common], g_own.at[:, rest]))
    loads = [pltpu.make_async_copy(src, dst, load.at[i]) for i, (src, dst) in enumerate(loads)]
    for copy in loads[:n_small]:
        copy.start()

    barrier = pltpu.get_barrier_semaphore()
    for dev in (up, down, across, twin, far):
        pl.semaphore_signal(barrier, inc=1, device_id=dev, device_id_type=MESH)

    def greet(k, carry):
        pl.semaphore_signal(barrier, inc=1, device_id=chip_dev(lax.rem(chip + k, chips)), device_id_type=MESH)
        return carry

    lax.fori_loop(1, chips, greet, 0)

    for copy in loads[n_small:]:
        copy.start()
    for copy in loads[:n_small]:
        copy.wait()
    shared_at = pl.ds(swap, shared)

    def weigh(p):
        for k in range(2):
            r = pl.ds((2 * k + p) * sub, sub)
            gath[p, 0, 0, k] = (q_own[r, :].astype(F32) * pc_own[...]).astype(BF16)
            px[p, k, :, 0:swap] = (q_oth[r, :].astype(F32) * pc_oth[...]).astype(BF16)
            px[p, k, :, shared_at] = gath[p, 0, 0, k, :, shared_at]

    weigh(0)
    pl.semaphore_wait(barrier, 5 + chips - 1)

    def wait_for(ref, sem):
        pltpu.make_async_copy(ref, ref, sem).wait()

    seen = set()
    whole = set()

    def block(p, place, o, k=None):
        return gath.at[p, place, o] if k is None else gath.at[p, place, o, k]

    def send(p, src, dst, o, k, dev):
        pltpu.make_async_remote_copy(
            src_ref=block(p, src, o, k), dst_ref=block(p, dst, o, k),
            send_sem=ag_send, recv_sem=ag_recv.at[p, dst, o, k or 0], device_id=dev, device_id_type=MESH,
        ).start()

    def arrived(p, place, o, k):
        k = None if (p, place, o) in whole else k
        if (p, place, o, k) not in seen and (place, o) != (0, 0):
            seen.add((p, place, o, k))
            wait_for(block(p, place, o, k), ag_recv.at[p, place, o, k or 0])

    def pass_on(o, hops, p, split=False):
        for dev, way, first in ((up, UP, 0), (down, DOWN, 1)):
            here = way[hops - 1] if hops else 0
            if hops == 3 or split:
                for k in (first, 1 - first) if hops < 3 else (first,):
                    arrived(p, here, o, k)
                    send(p, here, way[hops], o, k, dev)
            else:
                for k in range(2):
                    arrived(p, here, o, k)
                whole.add((p, way[hops], o))
                send(p, here, way[hops], o, None, dev)

    for p in range(2):
        if p == 1:
            weigh(1)
        pass_on(0, 0, p)
        whole.add((p, 0, 1))
        pltpu.make_async_remote_copy(
            src_ref=px.at[p], dst_ref=gath.at[p, 0, 1],
            send_sem=x_send, recv_sem=ag_recv.at[p, 0, 1, 0], device_id=across, device_id_type=MESH,
        ).start()
    for i in range(PIECES):
        loads[n_small + i].wait()
        r = pl.ds(i * piece, piece)
        pltpu.make_async_remote_copy(
            src_ref=g_send.at[r], dst_ref=g_oth.at[r],
            send_sem=gx_send, recv_sem=gx_recv.at[i], device_id=across, device_id_type=MESH,
        ).start()
    for copy in loads[n_small + PIECES :]:
        copy.wait()

    q_at = docs
    x_at = docs + EXTRA
    batches = []
    count = [0]

    def exchange(region, c0, c1):
        n = count[0]
        count[0] += 1
        p, d0, d1, o0, o1 = region
        window, places, sides = pl.ds(c0, c1 - c0), pl.ds(d0, d1 - d0), pl.ds(o0, o1 - o0)
        pltpu.make_async_remote_copy(
            src_ref=part.at[1 - core, p, places, sides, :, window], dst_ref=cx.at[p, places, sides, :, window],
            send_sem=cx_send, recv_sem=cx_recv.at[n], device_id=twin, device_id_type=MESH,
        ).start()
        batches[-1].append((n, region, c0, c1))

    def multiply(regions, own, x0, x1):
        blocks = []
        for p, d0, d1, o0, o1 in regions:
            for d in range(d0, d1):
                for o in range(o0, o1):
                    for k in range(2):
                        arrived(p, d, o, k)
            blocks.append(gath[p, d0:d1, o0:o1].reshape(-1, keep))
        flat = blocks[0] if len(blocks) == 1 else jnp.concatenate(blocks, axis=0)

        def store(value, c0, c1):
            at = 0
            for p, d0, d1, o0, o1 in regions:
                shape = (d1 - d0, o1 - o0, 2, sub, c1 - c0)
                size = math.prod(shape[:4])
                v = value[at : at + size].reshape(shape)
                at += size
                for k in range(2):
                    part[k, p, d0:d1, o0:o1, :, c0:c1] = v[:, :, k]

        if own:
            store(lax.dot_general(flat, g_own[...], NT, preferred_element_type=F32), 0, docs)
        if x1 > x0:
            weights = g_oth[x0 * piece : x1 * piece]
            dots = lax.dot_general(flat[:, :swap], weights, NT, preferred_element_type=F32)
            store(dots, x_at + x0 * piece, x_at + x1 * piece)
        if own:
            for p, d0, d1, o0, o1 in regions:
                for d in range(d0, d1):
                    for o in range(o0, o1):
                        for k in range(2):
                            v = gath[p, d, o, k].astype(F32)
                            if o == 1:
                                v = v[:, :swap]
                            sq = jnp.sum(v * v, axis=1, keepdims=True)
                            part[k, p, d, o, :, q_at:x_at] = jnp.broadcast_to(sq, (sub, EXTRA))
        batches.append([])
        for region in regions:
            exchange(region, 0 if own else x_at + x0 * piece, x_at + x1 * piece)

    done = [0]

    def high_low(sq):
        high = sq.astype(BF16).astype(F32)
        low = (sq - high).astype(BF16).astype(F32)
        lane = lax.broadcasted_iota(jnp.int32, sq.shape, sq.ndim - 1)
        return jnp.where(lane < EXTRA // 2, high, low).astype(BF16)

    def reduce_batch(batch):
        units_of = {}
        late = 1 if batch[0][1] in FAR else 0
        for n, (p, d0, d1, o0, o1), c0, c1 in batch:
            window, places, sides = pl.ds(c0, c1 - c0), pl.ds(d0, d1 - d0), pl.ds(o0, o1 - o0)
            wait_for(cx.at[p, places, sides, :, window], cx_recv.at[n])
            u0, u1 = 2 * p + o0, 2 * p + o1
            v = part[core, p, d0:d1, o0:o1, :, c0:c1] + cx[p, d0:d1, o0:o1, :, c0:c1]
            if c0 == 0:
                rs_out[d0:d1, u0:u1, :, 0:q_at] = v[..., :q_at].astype(BF16)
                rs_out[d0:d1, u0:u1, :, q_at:x_at] = high_low(v[..., q_at:x_at])
                if c1 > x_at:
                    rs_out[d0:d1, u0:u1, :, x_at:c1] = v[..., x_at:].astype(BF16)
            else:
                rs_out[d0:d1, u0:u1, :, c0:c1] = v.astype(BF16)
            for d in range(d0, d1):
                units_of.setdefault(d, []).append((u0, u1))
        window = pl.ds(c0, c1 - c0)
        for d in sorted(units_of, key=lambda d: -d):
            runs = []
            for u0, u1 in sorted(units_of[d]):
                if runs and runs[-1][1] == u0:
                    runs[-1] = (runs[-1][0], u1)
                else:
                    runs.append((u0, u1))
            owner = lax.rem(z + (OFFSETS[d] + n_z), n_z)

            @pl.when(owner != y)
            def _(d=d, runs=runs, owner=owner):
                for u0, u1 in runs:
                    units = pl.ds(u0, u1 - u0)
                    pltpu.make_async_remote_copy(
                        src_ref=rs_out.at[d, units, :, window], dst_ref=rs_in.at[y, units, :, window],
                        send_sem=rs_send, recv_sem=rs_recv.at[late],
                        device_id=chip_dev(x_hi * n_y + owner), device_id_type=MESH,
                    ).start()

            @pl.when(owner == y)
            def _(d=d, runs=runs):
                for u0, u1 in runs:
                    rs_in[y, u0:u1, :, c0:c1] = rs_out[d, u0:u1, :, c0:c1]

    def reduce_out(last=False):
        while done[0] < len(batches) - (0 if last else 1):
            reduce_batch(batches[done[0]])
            done[0] += 1

    def doc_squares():
        step = 64
        sums = []
        for i in range(docs // step):
            r = slice(i * step, (i + 1) * step)
            acc = jnp.zeros((step, 128), F32)
            for ref in (g_own, g_send):
                for k in range(ref.shape[1] // 128):
                    v = ref[r, k * 128 : (k + 1) * 128].astype(F32)
                    acc = acc + v * v
            sums.append(acc)
        lanes = jnp.concatenate(sums, axis=0)
        ones = jnp.ones((8, 128), F32)
        sq = lax.dot_general(ones, lanes, NT, preferred_element_type=F32, precision=lax.Precision.HIGHEST)
        ds_part[...] = sq[0:1]
        pltpu.make_async_remote_copy(
            src_ref=ds_part, dst_ref=ds_cx, send_sem=dsc_send, recv_sem=dsc_recv, device_id=twin, device_id_type=MESH
        ).start()

    def doc_spread():
        wait_for(ds_cx, dsc_recv)
        ds_out[...] = ds_part[...] + ds_cx[...]
        ds_in[chip] = ds_out[...]

        def spread(k, carry):
            pltpu.make_async_remote_copy(
                src_ref=ds_out, dst_ref=ds_in.at[chip], send_sem=ds_send, recv_sem=ds_recv,
                device_id=chip_dev(lax.rem(chip + k, chips)), device_id_type=MESH,
            ).start()
            return carry

        lax.fori_loop(1, chips, spread, 0)

    def piece_here(i):
        r = pl.ds(i * piece, piece)
        wait_for(g_oth.at[r], gx_recv.at[i])

    def sum_along_y(o, p):
        acc = rs_in[0, 2 * p + o].astype(F32)
        for k in range(1, n_y):
            acc = acc + rs_in[k, 2 * p + o].astype(F32)
        total[o, p * sub : (p + 1) * sub] = acc

    span = docs + EXTRA

    def send_along_x(o):
        v = total[o]
        sq = v[:, q_at : q_at + 1] + v[:, q_at + EXTRA // 2 : q_at + EXTRA // 2 + 1]
        fx_out[o, :, 0:q_at] = v[:, 0:q_at].astype(BF16)
        fx_out[o, :, q_at:x_at] = high_low(jnp.broadcast_to(sq, (2 * sub, EXTRA)))
        fx_out[o, :, x_at:] = v[:, x_at:].astype(BF16)
        owner_hi = lax.rem(col + o, 2)
        other = lax.rem(owner_hi + x_hi, 2)
        row_dev = 2 * (owner_hi * n_y + y) + core
        pltpu.make_async_remote_copy(
            src_ref=fx_out.at[o, :, pl.ds(q_at, span)], dst_ref=fx.at[2 * other],
            send_sem=fx_send, recv_sem=fx_recv.at[2 * other],
            device_id=(doc_at(1 - col, 0), row_dev), device_id_type=MESH,
        ).start()

        @pl.when(owner_hi != x_hi)
        def _():
            pltpu.make_async_remote_copy(
                src_ref=fx_out.at[o, :, pl.ds(0, span)], dst_ref=fx.at[1],
                send_sem=fx_send, recv_sem=fx_recv.at[1],
                device_id=(doc, row_dev), device_id_type=MESH,
            ).start()

    pass_on(0, 1, 0)
    pass_on(1, 0, 0)
    doc_squares()
    multiply([(0, 0, 1, 0, 2), (0, 1, 3, 0, 1), (1, 0, 1, 0, 2), (1, 1, 3, 0, 1)], True, 0, 0)
    doc_spread()
    pass_on(0, 2, 0)
    reduce_out(last=True)
    pass_on(1, 1, 0)
    multiply([(0, 3, 5, 0, 1), (0, 1, 3, 1, 2)], True, 0, 0)
    piece_here(0)
    multiply([(0, 0, 3, 0, 2), (0, 3, 5, 0, 1), (1, 0, 1, 0, 2), (1, 1, 3, 0, 1)], False, 0, 1)
    pass_on(0, 3, 0)
    reduce_out()
    pass_on(1, 2, 0)
    pass_on(0, 1, 1)
    reduce_out(last=True)
    multiply([(0, 5, 8, 0, 1), (0, 3, 5, 1, 2)], True, 0, 1)
    piece_here(1)
    multiply([(0, 0, 5, 0, 2), (0, 5, 8, 0, 1), (1, 0, 1, 0, 2), (1, 1, 3, 0, 1)], False, 1, 2)
    pass_on(1, 3, 0)
    pass_on(1, 0, 1)
    reduce_out()
    pass_on(0, 2, 1)
    reduce_out(last=True)
    multiply([(0, 5, 8, 1, 2), (1, 3, 5, 0, 1)], True, 0, 2)
    pass_on(1, 1, 1)
    reduce_out(last=True)
    piece_here(2)
    multiply([(0, 0, 8, 0, 2), (1, 0, 1, 0, 2), (1, 1, 5, 0, 1)], False, 2, 3)
    pass_on(0, 3, 1)
    reduce_out()
    multiply([(1, 1, 3, 1, 2), (1, 5, 7, 0, 1)], True, 0, 3)
    pass_on(1, 2, 1, split=True)
    reduce_out(last=True)
    multiply([(1, 3, 5, 1, 2), (1, 7, 8, 0, 1)], True, 0, 3)
    reduce_out()
    pass_on(1, 3, 1)
    piece_here(3)
    multiply([(0, 0, 8, 0, 2), (1, 0, 5, 0, 2), (1, 5, 8, 0, 1)], False, 3, 4)
    reduce_out(last=True)
    multiply([FAR[0]], True, 0, 4)
    reduce_out(last=True)
    multiply([FAR[1]], True, 0, 4)
    reduce_out(last=True)

    distance = lax.rem(y - z + 2 * n_y, n_y)
    far = jnp.logical_and(distance >= 3, distance <= n_y - 3)

    @pl.when(far)
    def _():
        wait_for(rs_in.at[pl.ds(0, n_y - 1), pl.ds(0, 3)], rs_recv.at[0])

    @pl.when(jnp.logical_not(far))
    def _():
        wait_for(rs_in.at[pl.ds(0, n_y - 1)], rs_recv.at[0])

    sum_along_y(0, 0)
    sum_along_y(0, 1)
    send_along_x(0)
    sum_along_y(1, 0)

    @pl.when(far)
    def _():
        wait_for(rs_in.at[pl.ds(0, n_y - 1), 3], rs_recv.at[1])

    sum_along_y(1, 1)
    send_along_x(1)
    wait_for(ds_in.at[pl.ds(0, chips - 1)], ds_recv)
    doc_total = jnp.sum(ds_in[...], axis=0)
    here = total[lax.rem(x_hi + col, 2), :, 0:span]
    for i in range(3):
        wait_for(fx.at[i], fx_recv.at[i])
    got = [fx[i].astype(F32) for i in range(3)]
    dots = here[:, :docs] + got[1][:, :docs] + got[0][:, EXTRA:] + got[2][:, EXTRA:]
    sq = here[:, docs:] + got[1][:, docs:] + got[0][:, :EXTRA] + got[2][:, :EXTRA]
    query_sq = sq[:, 0:1] + sq[:, EXTRA // 2 : EXTRA // 2 + 1]
    out_ref[...] = factor * dots * lax.rsqrt(query_sq + 1e-06) * lax.rsqrt(doc_total + 1e-06)

    wait_for(gath.at[:, pl.ds(0, 7)], ag_send)
    wait_for(px, x_send)
    wait_for(g_oth, gx_send)
    wait_for(cx, cx_send)
    wait_for(rs_out.at[pl.ds(0, n_y - 1)], rs_send)
    wait_for(fx, fx_send)
    wait_for(ds_cx, dsc_send)
    wait_for(ds_in.at[pl.ds(0, chips - 1)], ds_send)


def shards(grads, queries, precond):
    n_doc = lax.axis_size("doc")
    n_layer = lax.axis_size("layer")
    docs, width = grads.shape[0], grads.shape[2]
    rows = queries.shape[0]
    chips = n_layer // 2
    n_y = chips // 2
    own_rows = rows * n_doc // n_layer
    swap = width * 13 // 32
    keep = width - swap
    sub = rows // 4
    places = len(OFFSETS)
    wide = 2 * docs + EXTRA
    factor = math.sqrt(n_layer * width)
    dma = pltpu.SemaphoreType.DMA
    return pl.pallas_call(
        functools.partial(kernel, n_doc, n_layer, swap, factor),
        out_shape=jax.ShapeDtypeStruct((own_rows, docs), F32),
        in_specs=[pl.BlockSpec(memory_space=pltpu.HBM)] * 3,
        out_specs=pl.BlockSpec(memory_space=pltpu.VMEM),
        scratch_shapes=[
            pltpu.VMEM((docs, keep), BF16),
            pltpu.VMEM((docs, swap), BF16),
            pltpu.VMEM((docs, swap), BF16),
            pltpu.VMEM((rows, keep), BF16),
            pltpu.VMEM((rows, swap), BF16),
            pltpu.VMEM((1, keep), F32),
            pltpu.VMEM((1, swap), F32),
            pltpu.VMEM((2, places, 2, 2, sub, keep), BF16),
            pltpu.VMEM((2, 2, sub, keep), BF16),
            pltpu.VMEM((2, 2, places, 2, sub, wide), F32),
            pltpu.VMEM((2, places, 2, sub, wide), F32),
            pltpu.VMEM((places, 4, sub, wide), BF16),
            pltpu.VMEM((n_y, 4, sub, wide), BF16),
            pltpu.VMEM((2, 2 * sub, wide), F32),
            pltpu.VMEM((2, 2 * sub, wide), BF16),
            pltpu.VMEM((3, 2 * sub, docs + EXTRA), BF16),
            pltpu.VMEM((1, docs), F32),
            pltpu.VMEM((1, docs), F32),
            pltpu.VMEM((1, docs), F32),
            pltpu.VMEM((chips, 1, docs), F32),
            dma((8 + PIECES,)), dma, dma((2, places, 2, 2)), dma, dma, dma((PIECES,)), dma, dma((64,)),
            dma, dma((2,)), dma, dma((3,)), dma, dma, dma, dma,
        ],
        compiler_params=pltpu.CompilerParams(
            collective_id=0, has_side_effects=True, vmem_limit_bytes=63 << 20
        ),
        cost_estimate=pl.CostEstimate(
            flops=2 * rows * n_doc * docs * width, bytes_accessed=2 * docs * width, transcendentals=0
        ),
        name="gather_multiply_reduce",
    )(grads.reshape(docs, width), queries.reshape(rows, width), precond)


def solution(mesh):
    placed = (P("doc", "layer", None), P("doc", "layer", None), P("layer", None))
    return jax.shard_map(
        shards, mesh=mesh, in_specs=placed, out_specs=P("layer", "doc"), check_vma=False
    )
```
